128 devices in a mesh: tm: 4 (over x), space: 32 (over y, z, core).
Axes of the slice: x: 4, y: 4, z: 4, core: 2. Of those that a mesh axis runs over, the one named last changes fastest.
Arguments:
- slice_starts: float32 [4, 2, 64, 256, 256], P('tm', None, 'space'), may hold values from 0 to 1
- feed_rate: float32 [64, 256, 256], P('space'), may hold values from 0.01 to 0.1
- kill_rate: float32 [64, 256, 256], P('space'), may hold values from 0.03 to 0.12
Outputs:
- next_starts: float32 [4, 2, 64, 256, 256], P('tm', None, 'space')
The draws below stay inside these ranges and needn't reach their ends.
All inputs are finite; a program needn't handle non-finite values.
Results may differ from the reference program's by a relative error of at most 0.0001.
Values sent between devices are 32-bit elements; how exact they have to be, the bound alone decides.
No kernel may reach another device: no remote copies, remote signals or barrier semaphores. Data moves between devices by JAX's collectives and lax.ppermute only.
A program may use at most 128 MiB of HBM per device.

```python
import jax
import jax.numpy as jnp

NXY = 256
FSTEPS = 4
CSTEPS = 2
NZ = 64
SLICES = 4


def draw_slice_starts(key, part):
    key = jax.random.fold_in(key, 7)
    key_u, key_v = jax.random.split(key)
    shape = (SLICES, NZ, NXY, NXY)
    first = jax.random.uniform(key_u, shape, jnp.float32)
    second = jax.random.uniform(key_v, shape, jnp.float32)
    substrate = 0.6 + 0.4 * first * first
    catalyst = 0.4 * second * second
    return jnp.stack([substrate, catalyst], axis=1)


def levels(stream_key, dims, cuts, least, largest):
    loudness = 1.0
    for axis_at, shards_of in cuts:
        steps = jax.random.uniform(jax.random.fold_in(jax.random.fold_in(stream_key, 6), axis_at), (shards_of,), jnp.float32, least / len(cuts), largest / len(cuts))
        loudness = loudness * jnp.repeat(jnp.exp(steps), dims[axis_at] // shards_of).reshape((-1,) + (1,) * (len(dims) - 1 - axis_at))
    return loudness


def setup_inputs(seed: int = 0) -> dict:
    splits = jax.random.split(jax.random.key(seed), 4)
    return {
        "slice_starts": draw_slice_starts(jax.random.fold_in(splits[3], 71), 0),
        "feed_rate": jnp.clip(0.01 + 0.09 * jax.random.uniform(splits[1], (NZ, NXY, NXY), jnp.float32) ** levels(splits[1], (NZ, NXY, NXY), ((0, 32),), -0.2, 0.2), 0.01, 0.1),
        "kill_rate": jnp.clip(0.03 + 0.089999998 * jax.random.uniform(splits[2], (NZ, NXY, NXY), jnp.float32) ** levels(splits[2], (NZ, NXY, NXY), ((0, 32),), -0.2, 0.2), 0.03, 0.12),
    }


diff_u = 0.16
diff_v = 0.08


def laplacian(center, spacing):
    total = jnp.roll(center, -1, 3) + jnp.roll(center, 1, 3)
    total = total + jnp.roll(center, -1, 2) + jnp.roll(center, 1, 2)
    total = total + jnp.roll(center, -1, 1) + jnp.roll(center, 1, 1)
    return (total - 6.0 * center) / (spacing * spacing)


def rates(fields, feed_field, kill_field, spacing):
    lap_field = laplacian(fields, spacing)
    substrate = fields[0]
    catalyst = fields[1]
    uvv_term = substrate * catalyst * catalyst
    rate_u = diff_u * lap_field[0] - uvv_term + feed_field * (1.0 - substrate)
    rate_v = diff_v * lap_field[1] + uvv_term - (feed_field + kill_field) * catalyst
    return jnp.stack([rate_u, rate_v])


def restrict(field):
    shape = field.shape
    lead = shape[:-3]
    blocks = field.reshape(lead + (shape[-3] // 2, 2, shape[-2] // 2, 2, shape[-1] // 2, 2))
    return jnp.mean(blocks, axis=(-5, -3, -1))


def prolong(field):
    return jnp.repeat(jnp.repeat(jnp.repeat(field, 2, -3), 2, -2), 2, -1)


def fine_prop(current, feed_rate, kill_rate):
    for step_index in range(FSTEPS):
        first_rate = rates(current, feed_rate, kill_rate, 1.0)
        midpoint = current + 1.0 * first_rate
        second_rate = rates(midpoint, feed_rate, kill_rate, 1.0)
        current = current + 0.5 * (first_rate + second_rate)
    return current


def coarse_prop(current, coarse_feed, coarse_kill):
    for step_index in range(CSTEPS):
        current = current + 2.0 * rates(current, coarse_feed, coarse_kill, 2.0)
    return current


def reference(slice_starts, feed_rate, kill_rate):
    coarse_feed = restrict(feed_rate)
    coarse_kill = restrict(kill_rate)
    chained = restrict(slice_starts[0])
    results = []
    for slice_index in range(SLICES):
        start = slice_starts[slice_index]
        fine_end = fine_prop(start, feed_rate, kill_rate)
        coarse_end = restrict(fine_end)
        coarse_jump = coarse_end - coarse_prop(restrict(start), coarse_feed, coarse_kill)
        chained = coarse_prop(chained, coarse_feed, coarse_kill) + coarse_jump
        results.append(fine_end + prolong(chained - coarse_end))
    return jnp.stack(results)
```

```python
import functools

import jax
import jax.numpy as jnp
from jax import lax
from jax.experimental import pallas as pl
from jax.experimental.pallas import tpu as pltpu
from jax.sharding import PartitionSpec as P

FSTEPS = 4
CSTEPS = 2
DU = 0.16
DV = 0.08
FIRST = 22
TILES = 32
F32 = jnp.float32
HIGH = lax.Precision.HIGHEST
VMEM_LIMIT = 40 * 1024 * 1024


def splitter(transposed):
    r = lax.broadcasted_iota(jnp.int32, (256, 256), 0)
    c = lax.broadcasted_iota(jnp.int32, (256, 256), 1)
    if transposed:
        r, c = c, r
    return jnp.where(r == 2 * (c % 128) + c // 128, 1.0, 0.0).astype(F32)


def prep_kernel(parity, x, feed, kill, pair_a, pair_b, cross_a, cross_b, rows):
    mat = splitter(False)
    flip = parity[0]

    def scatter(plane, targets):
        done = jnp.dot(plane, mat, precision=HIGH, preferred_element_type=F32)
        rows[0] = done[:, :128]
        rows[1] = done[:, 128:]
        for i in range(TILES):
            for h in range(2):
                tile = rows[h, pl.ds(i, 8, stride=32), :]
                for (a, b), q in targets:
                    if i < FIRST:
                        a[q, i, h] = tile
                    else:
                        b[q, i - FIRST, h] = tile

    pair, cross = (pair_a, pair_b), (cross_a, cross_b)
    for sp in range(2):
        for q in range(2):
            scatter(x[sp, q ^ flip], [(pair, 2 * sp + q), (cross, 2 * sp + q)])
    for q, target in ((0, cross), (1, pair)):
        f = feed[q ^ flip]
        scatter(f, [(target, 4)])
        scatter(0.52 - (f + kill[q ^ flip]), [(target, 5)])


def prep(parity, x, feed, kill):
    a = jax.ShapeDtypeStruct((6, FIRST, 2, 8, 128), F32)
    b = jax.ShapeDtypeStruct((6, TILES - FIRST, 2, 8, 128), F32)
    vm = pl.BlockSpec(memory_space=pltpu.VMEM)
    return pl.pallas_call(
        prep_kernel,
        out_shape=[a, b, a, b],
        in_specs=[pl.BlockSpec(memory_space=pltpu.SMEM), vm, vm, vm],
        out_specs=[vm] * 4,
        scratch_shapes=[pltpu.VMEM((2, 256, 128), F32)],
        compiler_params=pltpu.CompilerParams(vmem_limit_bytes=VMEM_LIMIT),
        name="prep",
    )(parity, x, feed, kill)


ORDER = (1, 0, 2, 3, 5, 4)


def heun_kernel(step, second, total, *refs):
    refs = list(refs)
    groups = 2 if second else 1
    state = [refs[3 * g:3 * g + 3] for g in range(groups)]
    refs = refs[3 * groups:]
    rate = [refs[4 * g:4 * g + 4] for g in range(groups)]
    refs = refs[4 * groups:]
    out, cells, mids, coef, sems = refs
    copies = []

    def copy(src, dst):
        c = pltpu.make_async_copy(src, dst, sems.at[len(copies)])
        c.start()
        copies.append(c)

    lo = FIRST - 2 * step - 4 if second else 2 * step
    if second:
        na = FIRST - 4 * step
        pieces = [(0, na - 4, 0, 4), (1, 0, 4, total - 8), (0, 0, total - 4, 4)]
        rate_pieces = [(0, lo, 0, FIRST - lo), (1, 0, FIRST - lo, TILES - FIRST), (0, 0, TILES - lo, total - TILES + lo)]
    else:
        pieces = [(0, 0, 0, total)]
        rate_pieces = [(0, lo, 0, total)]
    for g, at, to, n in pieces:
        for ref, slot in zip(state[g], (2, 0, 4)):
            for sp in range(2):
                copy(ref.at[pl.ds(2 * sp, 2), pl.ds(at, n)], cells.at[sp, pl.ds(slot, 2), pl.ds(to, n)])
    for g, at, to, n in rate_pieces:
        sent_cross, sent_pair, got_cross, got_pair = rate[g]
        for ref, place in ((got_cross, 0), (sent_cross, 1), (sent_pair, 2), (got_pair, 3)):
            copy(ref.at[pl.ds(4, 2), pl.ds(at, n)], coef.at[:, place, pl.ds(to, n)])
    for c in copies:
        c.wait()
    if second:
        for sp in range(2):
            for slot in range(6):
                for j in range(total - 4, total):
                    for h in range(2):
                        cells[sp, slot, j, h] = pltpu.roll(cells[sp, slot, j, h], 7, 0)
            for place in range(4):
                for j in range(TILES - lo, total):
                    for h in range(2):
                        coef[sp, place, j, h] = pltpu.roll(coef[sp, place, j, h], 7, 0)

    def beside(here, other, h):
        return other + pltpu.roll(other, 1 if h == 0 else 127, 1)

    @pl.loop(1, total - 1)
    def _(j):
        mid = [[cells[sp, ORDER[p], j, h] for h in range(2)] for sp in range(2) for p in range(6)]
        for p in range(1, 5):
            for h in range(2):
                new = []
                for sp in range(2):
                    at = sp * 6 + p
                    slot = ORDER[p]
                    total6 = beside(None, mid[at][1 - h], h) + (cells[sp, slot, j - 1, h] + cells[sp, slot, j + 1, h])
                    total6 = total6 + (mid[at - 1][h] + mid[at + 1][h])
                    new.append(total6)
                u, v = mid[p][h], mid[6 + p][h]
                uvv = u * v * v
                f, cv = coef[0, p - 1, j, h], coef[1, p - 1, j, h]
                mids[0, p - 1, j, h] = DU * new[0] + (1.0 - 6.0 * DU) * u + f * (1.0 - u) - uvv
                mids[1, p - 1, j, h] = DV * new[1] + cv * v + uvv

    @pl.loop(2, total - 2)
    def _(j):
        mid = [[mids[sp, p, j, h] for h in range(2)] for sp in range(2) for p in range(4)]
        for p in range(1, 3):
            for h in range(2):
                new = []
                for sp in range(2):
                    at = sp * 4 + p
                    total6 = beside(None, mid[at][1 - h], h) + (mids[sp, p, j - 1, h] + mids[sp, p, j + 1, h])
                    total6 = total6 + (mid[at - 1][h] + mid[at + 1][h])
                    new.append(total6)
                u, v = mid[p][h], mid[4 + p][h]
                uvv = u * v * v
                f, cv = coef[0, p, j, h], coef[1, p, j, h]
                ru = DU * new[0] + (1.0 - 6.0 * DU) * u + f * (1.0 - u) - uvv
                rv = DV * new[1] + cv * v + uvv
                out[p - 1, j - 2, h] = 0.5 * (cells[0, p + 1, j, h] + ru)
                out[2 + p - 1, j - 2, h] = 0.5 * (cells[1, p + 1, j, h] + rv)


def heun(step, second, state, rate):
    total = (TILES - FIRST + 4 * step + 8) if second else FIRST - 4 * step
    groups = len(state)
    ins = [r for g in state for r in g] + [r for g in rate for r in g]
    copies = (18 + 12) if second else 10
    return pl.pallas_call(
        functools.partial(heun_kernel, step, second, total),
        out_shape=jax.ShapeDtypeStruct((4, total - 4, 2, 8, 128), F32),
        in_specs=[pl.BlockSpec(memory_space=pl.ANY)] * len(ins),
        out_specs=pl.BlockSpec(memory_space=pltpu.VMEM),
        scratch_shapes=[
            pltpu.VMEM((2, 6, total, 2, 8, 128), F32),
            pltpu.VMEM((2, 4, total, 2, 8, 128), F32),
            pltpu.VMEM((2, 4, total, 2, 8, 128), F32),
            pltpu.SemaphoreType.DMA((copies,)),
        ],
        compiler_params=pltpu.CompilerParams(vmem_limit_bytes=VMEM_LIMIT),
        cost_estimate=pl.CostEstimate(flops=total * 2048 * 150, bytes_accessed=total * 8192 * 20, transcendentals=0),
        name="heun_b%d" % step if second else "heun_a%d" % step,
    )(*ins)


def finish_kernel(parity, state, shift, out, rows):
    mat = splitter(True)
    flip = parity[0]
    for sp in range(2):
        for q in range(2):
            for i in range(TILES):
                for h in range(2):
                    rows[h, pl.ds(i, 8, stride=32), :] = state[2 * sp + q, i, h] + shift[sp, i // 2]
            both = jnp.concatenate([rows[0], rows[1]], axis=1)
            out[sp, q ^ flip] = jnp.dot(both, mat, precision=HIGH, preferred_element_type=F32)


def finish(parity, state, shift):
    vm = pl.BlockSpec(memory_space=pltpu.VMEM)
    return pl.pallas_call(
        finish_kernel,
        out_shape=jax.ShapeDtypeStruct((2, 2, 256, 256), F32),
        in_specs=[pl.BlockSpec(memory_space=pltpu.SMEM), vm, vm],
        out_specs=vm,
        scratch_shapes=[pltpu.VMEM((2, 256, 128), F32)],
        compiler_params=pltpu.CompilerParams(vmem_limit_bytes=VMEM_LIMIT),
        name="finish",
    )(parity, state, shift)


def swap_pair(x):
    n = lax.axis_size("space")
    return lax.ppermute(x, "space", [(i, i ^ 1) for i in range(n)])


def swap_cross(x):
    n = lax.axis_size("space")
    return lax.ppermute(x, "space", [(i, (i + 1) % n if i % 2 else (i - 1) % n) for i in range(n)])


def joined(a, b, lead):
    head = jnp.roll(b[:, TILES - FIRST + lead:], 1, -2)
    return jnp.concatenate([head, a, b[:, :TILES - FIRST + lead]], axis=1)


def restrict(state):
    return 0.125 * state.reshape(2, 2, 16, 2, 2, 8, 128).sum((1, 3, 4))


def coarse_step(c, cf, ccv):
    total = jnp.roll(c, 1, 3) + jnp.roll(c, -1, 3)
    up = jnp.concatenate([c[:, 1:], jnp.roll(c[:, :1], -1, 2)], axis=1)
    down = jnp.concatenate([jnp.roll(c[:, -1:], 1, 2), c[:, :-1]], axis=1)
    total = total + up + down + swap_pair(c) + swap_cross(c)
    lap = 0.25 * (total - 6.0 * c)
    u, v = c[0], c[1]
    uvv = u * v * v
    ru = DU * lap[0] - uvv + cf * (1.0 - u)
    rv = DV * lap[1] + uvv - ccv * v
    return c + 2.0 * jnp.stack([ru, rv])


def coarse_prop(c, cf, ccv):
    for _ in range(CSTEPS):
        c = coarse_step(c, cf, ccv)
    return c


def body(slice_starts, feed, kill):
    start = slice_starts[0]
    parity = (lax.axis_index("space") % 2).astype(jnp.int32).reshape(1)
    pair_a, pair_b, cross_a, cross_b = prep(parity, start, feed, kill)
    got_pair_a, got_cross_a = swap_pair(pair_a), swap_cross(cross_a)
    got_pair_b, got_cross_b = swap_pair(pair_b), swap_cross(cross_b)
    rate_a = (cross_a, pair_a, got_cross_a, got_pair_a)
    rate_b = (cross_b, pair_b, got_cross_b, got_pair_b)
    state_a = (pair_a, got_cross_a, got_pair_a)
    state_b = (pair_b, got_cross_b, got_pair_b)
    for step in range(FSTEPS):
        new_a = heun(step, False, [state_a], [rate_a])
        last = step == FSTEPS - 1
        if not last:
            next_a = (new_a, swap_cross(new_a), swap_pair(new_a))
        new_b = heun(step, True, [state_a, state_b], [rate_a, rate_b])
        if not last:
            state_a = next_a
            state_b = (new_b, swap_cross(new_b), swap_pair(new_b))
    fine = joined(new_a, new_b, 2 * FSTEPS)
    first = jnp.concatenate([pair_a[:4], pair_b[:4]], axis=1)
    f = jnp.concatenate([jnp.stack([cross_a[4:], pair_a[4:]], 1), jnp.stack([cross_b[4:], pair_b[4:]], 1)], axis=2)
    means = restrict(f)
    cf, ccv = means[0], 0.52 - means[1]
    coarse_end = restrict(fine)
    coarse_start = restrict(first)
    jump = coarse_end - coarse_prop(coarse_start, cf, ccv)
    index = lax.axis_index("tm")
    count = lax.axis_size("tm")
    jumps, starts = (
        lax.all_gather(jump[None], "tm", axis=0, tiled=True),
        lax.all_gather(coarse_start[None], "tm", axis=0, tiled=True),
    )
    walker = starts[0]
    chained = jnp.zeros_like(walker)
    for position in range(count):
        walker = coarse_prop(walker, cf, ccv) + jumps[position]
        chained = jnp.where(index == position, walker, chained)
    return finish(parity, fine, chained - coarse_end)[None]


def solution(mesh):
    in_specs = (P("tm", None, "space", None, None), P("space", None, None), P("space", None, None))
    out_specs = P("tm", None, "space", None, None)
    return jax.shard_map(body, mesh=mesh, in_specs=in_specs, out_specs=out_specs, check_vma=False)
```

```python
import functools

import jax
import jax.numpy as jnp
from jax import lax
from jax.experimental import pallas as pl
from jax.experimental.pallas import tpu as pltpu
from jax.sharding import PartitionSpec as P

FSTEPS = 4
CSTEPS = 2
DU = 0.16
DV = 0.08
FIRST = 22
TILES = 32
F32 = jnp.float32
UNROLL = 4
HIGH = lax.Precision.HIGHEST
VMEM_LIMIT = 40 * 1024 * 1024


def splitter(transposed):
    r = lax.broadcasted_iota(jnp.int32, (256, 256), 0)
    c = lax.broadcasted_iota(jnp.int32, (256, 256), 1)
    if transposed:
        r, c = c, r
    return jnp.where(r == 2 * (c % 128) + c // 128, 1.0, 0.0).astype(F32)


def prep_kernel(parity, x, feed, kill, pair_a, pair_b, cross_a, cross_b, rows):
    mat = splitter(False)
    flip = parity[0]

    def scatter(plane, targets):
        done = jnp.dot(plane, mat, precision=HIGH, preferred_element_type=F32)
        rows[0] = done[:, :128]
        rows[1] = done[:, 128:]
        for i in range(TILES):
            for h in range(2):
                tile = rows[h, pl.ds(i, 8, stride=32), :]
                for (a, b), q in targets:
                    if i < FIRST:
                        a[q, i, h] = tile
                    else:
                        b[q, i - FIRST, h] = tile

    pair, cross = (pair_a, pair_b), (cross_a, cross_b)
    for sp in range(2):
        for q in range(2):
            scatter(x[sp, q ^ flip], [(pair, 2 * sp + q), (cross, 2 * sp + q)])
    for q, target in ((0, cross), (1, pair)):
        f = feed[q ^ flip]
        scatter(f, [(target, 4)])
        scatter(0.52 - (f + kill[q ^ flip]), [(target, 5)])


def prep(parity, x, feed, kill):
    a = jax.ShapeDtypeStruct((6, FIRST, 2, 8, 128), F32)
    b = jax.ShapeDtypeStruct((6, TILES - FIRST, 2, 8, 128), F32)
    vm = pl.BlockSpec(memory_space=pltpu.VMEM)
    return pl.pallas_call(
        prep_kernel,
        out_shape=[a, b, a, b],
        in_specs=[pl.BlockSpec(memory_space=pltpu.SMEM), vm, vm, vm],
        out_specs=[vm] * 4,
        scratch_shapes=[pltpu.VMEM((2, 256, 128), F32)],
        compiler_params=pltpu.CompilerParams(vmem_limit_bytes=VMEM_LIMIT),
        name="prep",
    )(parity, x, feed, kill)


LINE = ((1, 1), (1, 0), (0, 0), (0, 1), (2, 1), (2, 0))


def runs(lo, hi, key):
    out = []
    for v in range(lo, hi):
        k = key(v)
        if out and out[-1][2] == k:
            out[-1][1] = v + 1
        else:
            out.append([v, v + 1, k])
    return out


def over(lo, hi, key, work):
    for start, stop, k in runs(lo, hi, key):
        if stop - start < 4:
            for v in range(start, stop):
                work(v, k)
        else:
            @pl.loop(start, stop, unroll=min(UNROLL, stop - start))
            def _(v):
                work(v, k)


def moved(x, rolled):
    return pltpu.roll(x, 7, 0) if rolled else x


def beside(other, h):
    return other + pltpu.roll(other, 1 if h == 0 else 127, 1)


def heun_kernel(step, second, total, after, *refs):
    refs = list(refs)
    groups = 2 if second else 1
    state = [refs[3 * g:3 * g + 3] for g in range(groups)]
    rate = [refs[3 * groups + 4 * g:3 * groups + 4 * g + 4] for g in range(groups)]
    out, mids = refs[-2:]
    lo = FIRST - 2 * step - 4 if second else 2 * step
    hi = lo + total

    def find_state(v):
        if not second:
            return 0, -2 * step, False
        if v < FIRST - 2 * step:
            return 0, -2 * step, False
        if v < TILES + 2 * step:
            return 1, 2 * step - FIRST, False
        return 0, -TILES - 2 * step, True

    def find_rate(v):
        if v < FIRST:
            return 0, 0, False
        if v < TILES:
            return 1, -FIRST, False
        return 0, -TILES, True

    def cell(sp, p, v, h, at):
        g, off, rolled = at
        source, plane = LINE[p]
        return moved(state[g][source][2 * sp + plane, v + off, h], rolled)

    def coef(k, place, v, h, at):
        g, off, rolled = at
        return moved(rate[g][(2, 0, 1, 3)[place]][4 + k, v + off, h], rolled)

    def ahead(u, v, near_u, near_v, f, cv):
        uvv = u * v * v
        return DU * near_u + (1.0 - 6.0 * DU) * u + f * (1.0 - u) - uvv, DV * near_v + cv * v + uvv

    def first(v, key):
        below, here, above, at = key
        c = [[cell(sp, p, v, h, here) for h in range(2)] for sp in range(2) for p in range(6)]
        for p in range(1, 5):
            for h in range(2):
                near = []
                for sp in range(2):
                    i = 6 * sp + p
                    s = cell(sp, p, v - 1, h, below) + cell(sp, p, v + 1, h, above)
                    near.append(beside(c[i][1 - h], h) + (s + (c[i - 1][h] + c[i + 1][h])))
                nu, nv = ahead(c[p][h], c[6 + p][h], *near, coef(0, p - 1, v, h, at), coef(1, p - 1, v, h, at))
                mids[0, p - 1, v - lo, h] = nu
                mids[1, p - 1, v - lo, h] = nv

    def then(v, key):
        here, at = key
        c = [[mids[sp, p, v - lo, h] for h in range(2)] for sp in range(2) for p in range(4)]
        for p in range(1, 3):
            for h in range(2):
                near = []
                for sp in range(2):
                    i = 4 * sp + p
                    s = mids[sp, p, v - lo - 1, h] + mids[sp, p, v - lo + 1, h]
                    near.append(beside(c[i][1 - h], h) + (s + (c[i - 1][h] + c[i + 1][h])))
                nu, nv = ahead(c[p][h], c[4 + p][h], *near, coef(0, p, v, h, at), coef(1, p, v, h, at))
                out[p - 1, v - lo - 2, h] = 0.5 * (cell(0, p + 1, v, h, here) + nu)
                out[2 + p - 1, v - lo - 2, h] = 0.5 * (cell(1, p + 1, v, h, here) + nv)

    over(lo + 1, hi - 1, lambda v: (find_state(v - 1), find_state(v), find_state(v + 1), find_rate(v)), first)
    over(lo + 2, hi - 2, lambda v: (find_state(v), find_rate(v)), then)


VM = pl.BlockSpec(memory_space=pltpu.VMEM)
SM = pl.BlockSpec(memory_space=pltpu.SMEM)
ANY = pl.BlockSpec(memory_space=pl.ANY)
PARAMS = pltpu.CompilerParams(vmem_limit_bytes=VMEM_LIMIT)
COARSE = (2, 16, 8, 128)


def heun(step, second, state, rate, after):
    total = (TILES - FIRST + 4 * step + 8) if second else FIRST - 4 * step
    ins = [r for g in state for r in g] + [r for g in rate for r in g]
    return pl.pallas_call(
        functools.partial(heun_kernel, step, second, total),
        out_shape=jax.ShapeDtypeStruct((4, total - 4, 2, 8, 128), F32),
        in_specs=[ANY] + [VM] * len(ins),
        out_specs=VM,
        scratch_shapes=[pltpu.VMEM((2, 4, total, 2, 8, 128), F32)],
        compiler_params=PARAMS,
        cost_estimate=pl.CostEstimate(flops=total * 2048 * 150, bytes_accessed=total * 8192 * 20, transcendentals=0),
        name="heun_b%d" % step if second else "heun_a%d" % step,
    )(after, *ins)


def mean_tile(tiles):
    s = [tiles[i] + tiles[i + 1] for i in range(0, 8, 2)]
    return 0.125 * ((s[0] + s[1]) + (s[2] + s[3]))


def mean_of(a, b, j, rows):
    ref, off = (a, 0) if 2 * j < FIRST else (b, FIRST)
    return mean_tile([ref[q, 2 * j + i - off, h] for q in rows for i in range(2) for h in range(2)])


def euler(get, cf, ccv, j):
    new = []
    for sp in range(2):
        c = get(0, sp, j)
        up = get(0, sp, j + 1) if j < 15 else pltpu.roll(get(0, sp, 0), 7, 0)
        down = get(0, sp, j - 1) if j else pltpu.roll(get(0, sp, 15), 1, 0)
        s = pltpu.roll(c, 1, 1) + pltpu.roll(c, 127, 1) + (up + down)
        new.append((c, s + (get(-1, sp, j) + get(1, sp, j))))
    (u, su), (v, sv) = new
    uvv = u * v * v
    nu = u + 2.0 * (0.25 * DU * (su - 6.0 * u) - uvv + cf * (1.0 - u))
    nv = v + 2.0 * (0.25 * DV * (sv - 6.0 * v) + uvv - ccv * v)
    return nu, nv


def own_first_kernel(pa, pb, ca, cb, gpa, gpb, gca, gcb, out, line):
    for j in range(16):
        for sp in range(2):
            rows = (2 * sp, 2 * sp + 1)
            line[0, sp, j] = mean_of(gca, gcb, j, rows)
            line[1, sp, j] = mean_of(pa, pb, j, rows)
            line[2, sp, j] = mean_of(gpa, gpb, j, rows)
        for k in range(2):
            (x, off), (y, _) = ((pa, 0), (ca, 0)) if 2 * j < FIRST else ((pb, FIRST), (cb, FIRST))
            tiles = [r[4 + k, 2 * j + i - off, h] for r in (y, x) for i in range(2) for h in range(2)]
            m = mean_tile(tiles)
            out[2 + k, j] = m if k == 0 else 0.52 - m
    for j in range(16):
        out[0, j], out[1, j] = euler(lambda d, sp, i: line[1 + d, sp, i], out[2, j], out[3, j], j)


def own_first(*refs):
    return pl.pallas_call(
        own_first_kernel,
        out_shape=jax.ShapeDtypeStruct((4, 16, 8, 128), F32),
        in_specs=[VM] * 8,
        out_specs=VM,
        scratch_shapes=[pltpu.VMEM((3,) + COARSE, F32)],
        compiler_params=PARAMS,
        name="own_first",
    )(*refs)


def jump_kernel(slot, a, b, here, cross, pair, end, send):
    line = (cross, here, pair)
    for j in range(16):
        g = euler(lambda d, sp, i: line[1 + d][sp, i], here[2, j], here[3, j], j)
        for sp in range(2):
            tiles = []
            for q in range(2):
                for i in range(2):
                    for h in range(2):
                        v = 2 * j + i
                        if v < 2 * FSTEPS:
                            x = pltpu.roll(b[2 * sp + q, v + TILES - FIRST + 2 * FSTEPS, h], 1, 0)
                        elif v < FIRST - 2 * FSTEPS:
                            x = a[2 * sp + q, v - 2 * FSTEPS, h]
                        else:
                            x = b[2 * sp + q, v - FIRST + 2 * FSTEPS, h]
                        tiles.append(x)
            m = mean_tile(tiles)
            end[sp, j] = m
            jump = m - g[sp]
            send[sp, j] = jnp.where(slot[0] == 0, g[sp] + jump, jump)


def jump_of(slot, a, b, here, cross, pair):
    shape = jax.ShapeDtypeStruct(COARSE, F32)
    return pl.pallas_call(
        jump_kernel,
        out_shape=[shape, shape],
        in_specs=[SM] + [VM] * 5,
        out_specs=[VM, VM],
        compiler_params=PARAMS,
        name="jump",
    )(slot, a, b, here, cross, pair)


def walk_kernel(both, near, far, q_own, q_cross, q_pair, q_far, jumps, out, mid):
    line = ((near, 1), (near, 0), (both, 0), (both, 1), (far, 0), (far, 1))
    rates = (q_cross, q_own, q_pair, q_far)
    for p in range(1, 5):
        for j in range(16):
            q = rates[p - 1]
            new = euler(lambda d, sp, i: line[p + d][0][line[p + d][1], sp, i], q[2, j], q[3, j], j)
            mid[p - 1, 0, j], mid[p - 1, 1, j] = new
    for p in range(1, 3):
        for j in range(16):
            q = rates[p]
            new = euler(lambda d, sp, i: mid[p + d, sp, i], q[2, j], q[3, j], j)
            for sp in range(2):
                out[p - 1, sp, j] = new[sp] + jumps[p - 1, sp, j]


def walk(*refs):
    return pl.pallas_call(
        walk_kernel,
        out_shape=jax.ShapeDtypeStruct((2,) + COARSE, F32),
        in_specs=[VM] * 8,
        out_specs=VM,
        scratch_shapes=[pltpu.VMEM((4,) + COARSE, F32)],
        compiler_params=PARAMS,
        name="walk",
    )(*refs)


def finish_kernel(parity, a, b, end, chained, out, rows):
    mat = splitter(True)
    flip = parity[0]
    for sp in range(2):
        shift = [chained[0, sp, j] - end[sp, j] for j in range(16)]
        for q in range(2):
            for v in range(TILES):
                for h in range(2):
                    if v < 2 * FSTEPS:
                        x = pltpu.roll(b[2 * sp + q, v + TILES - FIRST + 2 * FSTEPS, h], 1, 0)
                    elif v < FIRST - 2 * FSTEPS:
                        x = a[2 * sp + q, v - 2 * FSTEPS, h]
                    else:
                        x = b[2 * sp + q, v - FIRST + 2 * FSTEPS, h]
                    rows[h, pl.ds(v, 8, stride=32), :] = x + shift[v // 2]
            both = jnp.concatenate([rows[0], rows[1]], axis=1)
            out[sp, q ^ flip] = jnp.dot(both, mat, precision=HIGH, preferred_element_type=F32)


def finish(parity, a, b, end, chained):
    return pl.pallas_call(
        finish_kernel,
        out_shape=jax.ShapeDtypeStruct((2, 2, 256, 256), F32),
        in_specs=[SM] + [VM] * 4,
        out_specs=VM,
        scratch_shapes=[pltpu.VMEM((2, 256, 128), F32)],
        compiler_params=PARAMS,
        name="finish",
    )(parity, a, b, end, chained)


def swap_pair(x):
    n = lax.axis_size("space")
    return lax.ppermute(x, "space", [(i, i ^ 1) for i in range(n)])


def swap_cross(x):
    n = lax.axis_size("space")
    return lax.ppermute(x, "space", [(i, (i + 1) % n if i % 2 else (i - 1) % n) for i in range(n)])


def later(x, distance):
    n = lax.axis_size("tm")
    return lax.ppermute(x, "tm", [(i, i + distance) for i in range(n - distance)])


def body(slice_starts, feed, kill):
    start = slice_starts[0]
    parity = (lax.axis_index("space") % 2).astype(jnp.int32).reshape(1)
    index = lax.axis_index("tm").astype(jnp.int32)
    pair_a, pair_b, cross_a, cross_b = prep(parity, start, feed, kill)
    got_pair_a, got_cross_a = swap_pair(pair_a), swap_cross(cross_a)
    got_pair_b, got_cross_b = swap_pair(pair_b), swap_cross(cross_b)
    rate_a = (cross_a, pair_a, got_cross_a, got_pair_a)
    rate_b = (cross_b, pair_b, got_cross_b, got_pair_b)
    state_a = (pair_a, got_cross_a, got_pair_a)
    state_b = (pair_b, got_cross_b, got_pair_b)
    new_b = parity
    for step in range(FSTEPS):
        new_a = heun(step, False, [state_a], [rate_a], new_b)
        last = step == FSTEPS - 1
        if not last:
            next_a = (new_a, swap_cross(new_a), swap_pair(new_a))
        new_b = heun(step, True, [state_a, state_b], [rate_a, rate_b], new_a)
        if not last:
            state_a = next_a
            state_b = (new_b, swap_cross(new_b), swap_pair(new_b))
        if step == 0:
            q_own = own_first(pair_a, pair_b, cross_a, cross_b, got_pair_a, got_pair_b, got_cross_a, got_cross_b)
            q_cross = swap_cross(q_own)
            q_pair, q_far = swap_pair(q_own), swap_pair(q_cross)
    end, send = jump_of(index.reshape(1), new_a, new_b, q_own, q_cross, q_pair)
    from3, from2, from1 = later(send, 3), later(send, 2), later(send, 1)
    pick = lambda *xs: lax.select_n(index, *xs)
    first = pick(send, from1, from2, from3)
    jumps = jnp.stack([pick(send, send, from1, from2), pick(send, send, send, from1)])
    other_jumps = swap_pair(jumps)
    both = jnp.stack([first, swap_pair(first)])
    chained = [both]
    for position in range(lax.axis_size("tm") - 1):
        near = swap_cross(both)
        far = swap_pair(near)
        if position < 2:
            jump = jnp.stack([jumps[position], other_jumps[position]])
        else:
            jump = jnp.stack([send, send])
        both = walk(both, near, far, q_own, q_cross, q_pair, q_far, jump)
        chained.append(both)
    return finish(parity, new_a, new_b, end, pick(*chained))[None]


def solution(mesh):
    in_specs = (P("tm", None, "space", None, None), P("space", None, None), P("space", None, None))
    out_specs = P("tm", None, "space", None, None)
    return jax.shard_map(body, mesh=mesh, in_specs=in_specs, out_specs=out_specs, check_vma=False)
```

```python
import functools

import jax
import jax.numpy as jnp
from jax import lax
from jax.experimental import pallas as pl
from jax.experimental.pallas import tpu as pltpu
from jax.sharding import PartitionSpec as P

FSTEPS = 4
CSTEPS = 2
DU = 0.16
DV = 0.08
FIRST = 24
TILES = 32
F32 = jnp.float32
UNROLL = 8
VMEM_LIMIT = 16 * 1024 * 1024

VM = pl.BlockSpec(memory_space=pltpu.VMEM)
ANY = pl.BlockSpec(memory_space=pl.ANY)
PARAMS = pltpu.CompilerParams(vmem_limit_bytes=VMEM_LIMIT)
COARSE = (2, 16, 8, 128)
FLAT = 3
TAIL = 4 * (FIRST - 4 * FLAT) * 2


def splitter(transposed):
    r = lax.broadcasted_iota(jnp.int32, (256, 256), 0)
    c = lax.broadcasted_iota(jnp.int32, (256, 256), 1)
    if transposed:
        r, c = c, r
    return jnp.where(r == 2 * (c % 128) + c // 128, 1.0, 0.0).astype(jnp.bfloat16)


def permuted(x, mat):
    high = x.astype(jnp.bfloat16)
    rest = x - high.astype(F32)
    mid = rest.astype(jnp.bfloat16)
    low = (rest - mid.astype(F32)).astype(jnp.bfloat16)
    dot = lambda p: jnp.dot(p, mat, preferred_element_type=F32)
    return dot(high) + (dot(mid) + dot(low))


def odd():
    return lax.rem(lax.axis_index("space"), 2)


def prep_kernel(x, feed, kill, pair_a, pair_b, cross_a, cross_b, xs, rs, rows, sems):
    flip = odd()
    copies = []
    for i, (src, dst) in enumerate(
        [(x.at[sp, q], xs.at[2 * sp + q]) for sp in range(2) for q in range(2)]
        + [(src.at[q], rs.at[2 * k + q]) for q in range(2) for k, src in enumerate((feed, kill))]
    ):
        copies.append(pltpu.make_async_copy(src, dst, sems.at[i]))
        copies[-1].start()
    mat = splitter(False)

    def scatter(plane, k, targets):
        done = permuted(plane, mat)
        rows[k, 0] = done[:, :128]
        rows[k, 1] = done[:, 128:]
        for i in range(TILES):
            for h in range(2):
                tile = rows[k, h, pl.ds(i, 8, stride=32), :]
                for (a, b), q in targets:
                    if i < FIRST:
                        a[q, i, h] = tile
                    else:
                        b[q, i - FIRST, h] = tile

    pair, cross = (pair_a, pair_b), (cross_a, cross_b)
    for sp in range(2):
        copies[2 * sp].wait()
        copies[2 * sp + 1].wait()
        for q in range(2):
            scatter(xs[2 * sp + (q ^ flip)], 2 * sp + q, [(pair, 2 * sp + q), (cross, 2 * sp + q)])
    for c in copies[4:]:
        c.wait()
    for q, target in ((0, cross), (1, pair)):
        f = rs[q ^ flip]
        scatter(f, 4 + 2 * q, [(target, 4)])
        scatter(0.52 - (f + rs[2 + (q ^ flip)]), 5 + 2 * q, [(target, 5)])


def prep(x, feed, kill):
    a = jax.ShapeDtypeStruct((6, FIRST, 2, 8, 128), F32)
    b = jax.ShapeDtypeStruct((6, TILES - FIRST, 2, 8, 128), F32)
    hbm = pl.BlockSpec(memory_space=pltpu.HBM)
    return pl.pallas_call(
        prep_kernel,
        out_shape=[a, b, a, b],
        in_specs=[hbm] * 3,
        out_specs=[VM] * 4,
        scratch_shapes=[
            pltpu.VMEM((4, 256, 256), F32),
            pltpu.VMEM((4, 256, 256), F32),
            pltpu.VMEM((8, 2, 256, 128), F32),
            pltpu.SemaphoreType.DMA((8,)),
        ],
        compiler_params=PARAMS,
        name="prep",
    )(x, feed, kill)


LINE = ((1, 1), (1, 0), (0, 0), (0, 1), (2, 1), (2, 0))


def runs(lo, hi, key):
    out = []
    for v in range(lo, hi):
        k = key(v)
        if out and out[-1][2] == k:
            out[-1][1] = v + 1
        else:
            out.append([v, v + 1, k])
    return out


def over(lo, hi, key, work):
    for start, stop, k in runs(lo, hi, key):
        if stop - start < 4:
            for v in range(start, stop):
                work(v, k)
        else:
            @pl.loop(start, stop, unroll=min(UNROLL, stop - start))
            def _(v):
                work(v, k)


def moved(x, rolled):
    return pltpu.roll(x, 7, 0) if rolled else x


def beside(other, h):
    return other + pltpu.roll(other, 1 if h == 0 else 127, 1)


def heun_kernel(step, second, total, after, *refs):
    refs = list(refs)
    extra = refs.pop(0) if step == FLAT - 1 and not second else None
    groups = 2 if second else 1
    state = [refs[3 * g:3 * g + 3] for g in range(groups)]
    rate = [refs[3 * groups + 4 * g:3 * groups + 4 * g + 4] for g in range(groups)]
    out, mids = refs[-2:]
    lo = FIRST - 2 * step - 4 if second else 2 * step
    hi = lo + total

    def find_state(v):
        if not second:
            return 0, -2 * step, False
        if v < FIRST - 2 * step:
            return 0, -2 * step, False
        if v < TILES + 2 * step:
            return 1, 2 * step - FIRST, False
        return 0, -TILES - 2 * step, True

    def find_rate(v):
        if v < FIRST:
            return 0, 0, False
        if v < TILES:
            return 1, -FIRST, False
        return 0, -TILES, True

    def cell(sp, p, v, h, at):
        g, off, rolled = at
        source, plane = LINE[p]
        ref, q = state[g][source], 2 * sp + plane
        if g == 0 and step == FLAT:
            return moved(ref[(q * (FIRST - 4 * step) + v + off) * 2 + h], rolled)
        return moved(ref[q, v + off, h], rolled)

    def put(q, i, h, x):
        if extra is None:
            out[q, i, h] = x
        else:
            out[(q * (total - 4) + i) * 2 + h] = x

    def coef(k, place, v, h, at):
        g, off, rolled = at
        return moved(rate[g][(2, 0, 1, 3)[place]][4 + k, v + off, h], rolled)

    def ahead(u, v, near_u, near_v, f, cv):
        uvv = u * v * v
        return DU * near_u + (1.0 - 6.0 * DU) * u + f * (1.0 - u) - uvv, DV * near_v + cv * v + uvv

    def first(v, key):
        below, here, above, at = key
        c = [[cell(sp, p, v, h, here) for h in range(2)] for sp in range(2) for p in range(6)]
        for p in range(1, 5):
            for h in range(2):
                near = []
                for sp in range(2):
                    i = 6 * sp + p
                    s = cell(sp, p, v - 1, h, below) + cell(sp, p, v + 1, h, above)
                    near.append(beside(c[i][1 - h], h) + (s + (c[i - 1][h] + c[i + 1][h])))
                nu, nv = ahead(c[p][h], c[6 + p][h], *near, coef(0, p - 1, v, h, at), coef(1, p - 1, v, h, at))
                mids[0, p - 1, v - lo, h] = nu
                mids[1, p - 1, v - lo, h] = nv

    def then(v, key):
        here, at = key
        c = [[mids[sp, p, v - lo, h] for h in range(2)] for sp in range(2) for p in range(4)]
        for p in range(1, 3):
            for h in range(2):
                near = []
                for sp in range(2):
                    i = 4 * sp + p
                    s = mids[sp, p, v - lo - 1, h] + mids[sp, p, v - lo + 1, h]
                    near.append(beside(c[i][1 - h], h) + (s + (c[i - 1][h] + c[i + 1][h])))
                nu, nv = ahead(c[p][h], c[4 + p][h], *near, coef(0, p, v, h, at), coef(1, p, v, h, at))
                put(p - 1, v - lo - 2, h, 0.5 * (cell(0, p + 1, v, h, here) + nu))
                put(2 + p - 1, v - lo - 2, h, 0.5 * (cell(1, p + 1, v, h, here) + nv))

    if extra is not None:
        for k in range(4):
            for j in range(16):
                out[TAIL + 16 * k + j] = extra[k, j]

    over(lo + 1, hi - 1, lambda v: (find_state(v - 1), find_state(v), find_state(v + 1), find_rate(v)), first)
    over(lo + 2, hi - 2, lambda v: (find_state(v), find_rate(v)), then)


def heun(step, second, state, rate, after, extra=None):
    total = (TILES - FIRST + 4 * step + 8) if second else FIRST - 4 * step
    ins = [r for g in state for r in g] + [r for g in rate for r in g]
    shape = (4, total - 4, 2, 8, 128)
    if extra is not None:
        ins = [extra] + ins
        shape = (TAIL + 64, 8, 128)
    return pl.pallas_call(
        functools.partial(heun_kernel, step, second, total),
        out_shape=jax.ShapeDtypeStruct(shape, F32),
        in_specs=[ANY] + [VM] * len(ins),
        out_specs=VM,
        scratch_shapes=[pltpu.VMEM((2, 4, total, 2, 8, 128), F32)],
        compiler_params=PARAMS,
        cost_estimate=pl.CostEstimate(flops=total * 2048 * 150, bytes_accessed=total * 8192 * 20, transcendentals=0),
        name="heun_b%d" % step if second else "heun_a%d" % step,
    )(after, *ins)


def mean_tile(tiles):
    s = [tiles[i] + tiles[i + 1] for i in range(0, 8, 2)]
    return 0.125 * ((s[0] + s[1]) + (s[2] + s[3]))


def mean_of(a, b, j, rows):
    ref, off = (a, 0) if 2 * j < FIRST else (b, FIRST)
    return mean_tile([ref[q, 2 * j + i - off, h] for q in rows for i in range(2) for h in range(2)])


def euler(get, cf, ccv, j):
    new = []
    for sp in range(2):
        c = get(0, sp, j)
        up = get(0, sp, j + 1) if j < 15 else pltpu.roll(get(0, sp, 0), 7, 0)
        down = get(0, sp, j - 1) if j else pltpu.roll(get(0, sp, 15), 1, 0)
        s = pltpu.roll(c, 1, 1) + pltpu.roll(c, 127, 1) + (up + down)
        new.append((c, s + (get(-1, sp, j) + get(1, sp, j))))
    (u, su), (v, sv) = new
    uvv = u * v * v
    nu = u + 2.0 * (0.25 * DU * (su - 6.0 * u) - uvv + cf * (1.0 - u))
    nv = v + 2.0 * (0.25 * DV * (sv - 6.0 * v) + uvv - ccv * v)
    return nu, nv


def own_first_kernel(pa, pb, ca, cb, gpa, gpb, gca, gcb, out, line):
    for j in range(16):
        for sp in range(2):
            rows = (2 * sp, 2 * sp + 1)
            line[0, sp, j] = mean_of(gca, gcb, j, rows)
            line[1, sp, j] = mean_of(pa, pb, j, rows)
            line[2, sp, j] = mean_of(gpa, gpb, j, rows)
        for k in range(2):
            (x, off), (y, _) = ((pa, 0), (ca, 0)) if 2 * j < FIRST else ((pb, FIRST), (cb, FIRST))
            tiles = [r[4 + k, 2 * j + i - off, h] for r in (y, x) for i in range(2) for h in range(2)]
            m = mean_tile(tiles)
            out[2 + k, j] = m if k == 0 else 0.52 - m
    for j in range(16):
        out[0, j], out[1, j] = euler(lambda d, sp, i: line[1 + d, sp, i], out[2, j], out[3, j], j)


def own_first(*refs):
    return pl.pallas_call(
        own_first_kernel,
        out_shape=jax.ShapeDtypeStruct((4, 16, 8, 128), F32),
        in_specs=[VM] * 8,
        out_specs=VM,
        scratch_shapes=[pltpu.VMEM((3,) + COARSE, F32)],
        compiler_params=PARAMS,
        name="own_first",
    )(*refs)


def fine_tile(a, b, q, v, h):
    if v < 2 * FSTEPS:
        return pltpu.roll(b[q, v + TILES - FIRST + 2 * FSTEPS, h], 1, 0)
    if v < FIRST - 2 * FSTEPS:
        return a[q, v - 2 * FSTEPS, h]
    return b[q, v - FIRST + 2 * FSTEPS, h]


def jump_kernel(a, b, here, cross, pair, end, send, rate_cross, rate_pair):
    first = lax.axis_index("tm") == 0
    for k in range(2):
        for j in range(16):
            rate_cross[k, j] = cross[TAIL + 16 * (2 + k) + j]
            rate_pair[k, j] = pair[TAIL + 16 * (2 + k) + j]

    def get(d, sp, j):
        return here[sp, j] if d == 0 else (cross if d < 0 else pair)[TAIL + 16 * sp + j]

    for j in range(16):
        g = euler(get, here[2, j], here[3, j], j)
        for sp in range(2):
            m = mean_tile([fine_tile(a, b, 2 * sp + q, 2 * j + i, h) for q in range(2) for i in range(2) for h in range(2)])
            end[sp, j] = m
            jump = m - g[sp]
            send[sp, j] = jnp.where(first, g[sp] + jump, jump)


def jump_of(a, b, here, cross, pair):
    shape = jax.ShapeDtypeStruct(COARSE, F32)
    return pl.pallas_call(
        jump_kernel,
        out_shape=[shape] * 4,
        in_specs=[VM] * 5,
        out_specs=[VM] * 4,
        compiler_params=PARAMS,
        name="jump",
    )(a, b, here, cross, pair)


def pack_kernel(after, one, other, out):
    out[0] = one[...]
    out[1] = other[...]


def pack(one, other, after):
    return pl.pallas_call(
        pack_kernel,
        out_shape=jax.ShapeDtypeStruct((2,) + COARSE, F32),
        in_specs=[ANY, VM, VM],
        out_specs=VM,
        compiler_params=PARAMS,
        name="pack",
    )(after, one, other)


def walk_kernel(least, both, near, far, q_own, r_cross, r_pair, r_far, *refs):
    *jumps, out, mid = refs
    line = ((near, 1), (near, 0), (both, 0), (both, 1), (far, 0), (far, 1))
    rates = ((r_cross, 0), (q_own, 2), (r_pair, 0), (r_far, 0))
    counts = lax.axis_index("tm") >= least
    for p in range(1, 5):
        q, k = rates[p - 1]
        for j in range(16):
            new = euler(lambda d, sp, i: line[p + d][0][line[p + d][1], sp, i], q[k, j], q[k + 1, j], j)
            mid[p - 1, 0, j], mid[p - 1, 1, j] = new
    for n, jump in enumerate(jumps):
        q, k = rates[n + 1]
        for j in range(16):
            new = euler(lambda d, sp, i: mid[n + 1 + d, sp, i], q[k, j], q[k + 1, j], j)
            for sp in range(2):
                x = jnp.where(counts, new[sp], 0.0) + jump[sp, j]
                if len(jumps) == 2:
                    out[n, sp, j] = x
                else:
                    out[sp, j] = x


def walk(least, both, near, far, rates, jumps):
    return pl.pallas_call(
        functools.partial(walk_kernel, least),
        out_shape=jax.ShapeDtypeStruct(((2,) if len(jumps) == 2 else ()) + COARSE, F32),
        in_specs=[VM] * (7 + len(jumps)),
        out_specs=VM,
        scratch_shapes=[pltpu.VMEM((4,) + COARSE, F32)],
        compiler_params=PARAMS,
        name="walk%d" % least,
    )(both, near, far, *rates, *jumps)


def finish_kernel(a, b, end, chained, out, rows, done, sems):
    mat = splitter(True)
    flip = odd()
    copies = []
    for sp in range(2):
        shift = [chained[sp, j] - end[sp, j] for j in range(16)]
        for q in range(2):
            k = 2 * sp + q
            for v in range(TILES):
                for h in range(2):
                    rows[k, h, pl.ds(v, 8, stride=32), :] = fine_tile(a, b, k, v, h) + shift[v // 2]
            done[k] = permuted(jnp.concatenate([rows[k, 0], rows[k, 1]], axis=1), mat)
            copies.append(pltpu.make_async_copy(done.at[k], out.at[sp, q ^ flip], sems.at[k]))
            copies[-1].start()
    for c in copies:
        c.wait()


def finish(a, b, end, chained):
    return pl.pallas_call(
        finish_kernel,
        out_shape=jax.ShapeDtypeStruct((2, 2, 256, 256), F32),
        in_specs=[VM] * 4,
        out_specs=pl.BlockSpec(memory_space=pltpu.HBM),
        scratch_shapes=[
            pltpu.VMEM((4, 2, 256, 128), F32),
            pltpu.VMEM((4, 256, 256), F32),
            pltpu.SemaphoreType.DMA((4,)),
        ],
        compiler_params=PARAMS,
        name="finish",
    )(a, b, end, chained)


def swap_pair(x):
    n = lax.axis_size("space")
    return lax.ppermute(x, "space", [(i, i ^ 1) for i in range(n)])


def swap_cross(x):
    n = lax.axis_size("space")
    return lax.ppermute(x, "space", [(i, (i + 1) % n if i % 2 else (i - 1) % n) for i in range(n)])


def later(x, distance):
    n = lax.axis_size("tm")
    return lax.ppermute(x, "tm", [(i, i + distance) for i in range(n - distance)])


def body(slice_starts, feed, kill):
    pair_a, pair_b, cross_a, cross_b = prep(slice_starts[0], feed, kill)
    got_pair_a, got_cross_a = swap_pair(pair_a), swap_cross(cross_a)
    got_pair_b, got_cross_b = swap_pair(pair_b), swap_cross(cross_b)
    rate_a = (cross_a, pair_a, got_cross_a, got_pair_a)
    rate_b = (cross_b, pair_b, got_cross_b, got_pair_b)
    state_a = (pair_a, got_cross_a, got_pair_a)
    state_b = (pair_b, got_cross_b, got_pair_b)
    new_b = pair_b
    q_own = own_first(pair_a, pair_b, cross_a, cross_b, got_pair_a, got_pair_b, got_cross_a, got_cross_b)
    for step in range(FSTEPS):
        new_a = heun(step, False, [state_a], [rate_a], new_b, q_own if step == FLAT - 1 else None)
        last = step == FSTEPS - 1
        if not last:
            next_a = (new_a, swap_cross(new_a), swap_pair(new_a))
        new_b = heun(step, True, [state_a, state_b], [rate_a, rate_b], new_a)
        if not last:
            state_a = next_a
            state_b = (new_b, swap_cross(new_b), swap_pair(new_b))
    end, send, rate_cross, rate_pair = jump_of(new_a, new_b, q_own, state_a[1], state_a[2])
    rates = (q_own, rate_cross, rate_pair, swap_pair(rate_cross))
    from3, from2, from1 = later(send, 3), later(send, 2), later(send, 1)
    both = pack(from3, swap_pair(from3), rates[3])
    for least, jumps in ((3, (from2, swap_pair(from2))), (2, (from1, swap_pair(from1))), (1, (send,))):
        near = swap_cross(both)
        far = swap_pair(near)
        both = walk(least, both, near, far, rates, jumps)
    return finish(new_a, new_b, end, both)[None]


def solution(mesh):
    in_specs = (P("tm", None, "space", None, None), P("space", None, None), P("space", None, None))
    out_specs = P("tm", None, "space", None, None)
    return jax.shard_map(body, mesh=mesh, in_specs=in_specs, out_specs=out_specs, check_vma=False)
```

```python
import functools

import jax
import jax.numpy as jnp
from jax import lax
from jax.experimental import pallas as pl
from jax.experimental.pallas import tpu as pltpu
from jax.sharding import PartitionSpec as P

FSTEPS = 4
CSTEPS = 2
DU = 0.16
DV = 0.08
CUTS = (0, 18, 26, 32)
TILES = 32
STRIDE = 33
CHUNKS = len(CUTS) - 1
F32 = jnp.float32
UNROLL = 8
VMEM_LIMIT = 16 * 1024 * 1024

VM = pl.BlockSpec(memory_space=pltpu.VMEM)
ANY = pl.BlockSpec(memory_space=pl.ANY)
PARAMS = pltpu.CompilerParams(vmem_limit_bytes=VMEM_LIMIT)
COARSE = (2, 16, 8, 128)
PACK_COST = 10**10
COST = ((2 * 10**9,) * 4, (2 * 10**9,) * 2 + (4 * 10**9,) * 2, (2 * 10**9,) * 4)
FLAT = 3
TAIL = 4 * (CUTS[1] - 4 * FLAT) * 2


def splitter(transposed):
    r = lax.broadcasted_iota(jnp.int32, (256, 256), 0)
    c = lax.broadcasted_iota(jnp.int32, (256, 256), 1)
    if transposed:
        r, c = c, r
    return jnp.where(r == 2 * (c % 128) + c // 128, 1.0, 0.0).astype(jnp.bfloat16)


def permuted(x, mat):
    high = x.astype(jnp.bfloat16)
    rest = x - high.astype(F32)
    mid = rest.astype(jnp.bfloat16)
    low = (rest - mid.astype(F32)).astype(jnp.bfloat16)
    dot = lambda p: jnp.dot(p, mat, preferred_element_type=F32)
    return dot(high) + (dot(mid) + dot(low))


def odd():
    return lax.rem(lax.axis_index("space"), 2)


def chunk_of(v):
    return max(c for c in range(CHUNKS) if CUTS[c] <= v)


def scatter(plane, rows, mat, targets):
    done = permuted(plane, mat)
    for band in range(8):
        for h in range(2):
            rows[h, pl.ds(STRIDE * band, TILES), :] = done[TILES * band:TILES * (band + 1), 128 * h:128 * (h + 1)]
    for i in range(TILES):
        c = chunk_of(i)
        for h in range(2):
            tile = rows[h, pl.ds(i, 8, stride=STRIDE), :]
            for refs, q in targets:
                refs[c][q, i - CUTS[c], h] = tile


def prep_kernel(x, *refs):
    pair, cross, rows = refs[:CHUNKS], refs[CHUNKS:2 * CHUNKS], refs[-1]
    flip = odd()
    mat = splitter(False)
    for sp in range(2):
        for q in range(2):
            k = 2 * sp + q
            scatter(x[sp, q ^ flip], rows.at[k], mat, [(pair, k), (cross, k)])


def prep_rates_kernel(feed, kill, *refs):
    pair, cross, rows = refs[2 * CHUNKS:3 * CHUNKS], refs[3 * CHUNKS:4 * CHUNKS], refs[-1]
    flip = odd()
    mat = splitter(False)
    for q, target in ((0, cross), (1, pair)):
        f = feed[q ^ flip]
        scatter(f, rows.at[2 * q], mat, [(target, 4)])
        scatter(0.52 - (f + kill[q ^ flip]), rows.at[2 * q + 1], mat, [(target, 5)])


def prep(x, feed, kill):
    shapes = [jax.ShapeDtypeStruct((6, CUTS[c + 1] - CUTS[c], 2, 8, 128), F32) for c in range(CHUNKS)] * 2
    scratch = [pltpu.VMEM((4, 2, 8 * STRIDE, 128), F32)]
    sent = pl.pallas_call(
        prep_kernel,
        out_shape=shapes,
        in_specs=[VM],
        out_specs=[VM] * (2 * CHUNKS),
        scratch_shapes=scratch,
        compiler_params=PARAMS,
        name="prep",
    )(x)
    return pl.pallas_call(
        prep_rates_kernel,
        out_shape=shapes,
        in_specs=[VM, VM] + [VM] * (2 * CHUNKS),
        out_specs=[VM] * (2 * CHUNKS),
        scratch_shapes=scratch,
        input_output_aliases={2 + i: i for i in range(2 * CHUNKS)},
        compiler_params=PARAMS,
        name="prep_rates",
    )(feed, kill, *sent)


LINE = ((1, 1), (1, 0), (0, 0), (0, 1), (2, 1), (2, 0))


def runs(lo, hi, key):
    out = []
    for v in range(lo, hi):
        k = key(v)
        if out and out[-1][2] == k:
            out[-1][1] = v + 1
        else:
            out.append([v, v + 1, k])
    return out


def over(lo, hi, key, work):
    for start, stop, k in runs(lo, hi, key):
        if stop - start < 4:
            for v in range(start, stop):
                work(v, k)
        else:
            @pl.loop(start, stop, unroll=min(UNROLL, stop - start))
            def _(v):
                work(v, k)


def moved(x, rolled):
    return pltpu.roll(x, 7, 0) if rolled else x


def beside(other, h):
    return other + pltpu.roll(other, 1 if h == 0 else 127, 1)


def edges(step, c):
    lo = CUTS[c] + (2 * step if c == 0 else -2 * step)
    return lo, CUTS[c + 1] + (2 * step if c == CHUNKS - 1 else -2 * step)


def heun_kernel(step, c, after, *refs):
    refs = list(refs)
    extra = refs.pop(0) if step == FLAT - 1 and c == 0 else None
    state = [refs[3 * g:3 * g + 3] for g in range(c + 1)]
    refs = refs[3 * (c + 1):]
    rate = [refs[4 * g:4 * g + 4] for g in range(c + 1)]
    out, mids = refs[-2:]
    lo, hi = edges(step + 1, c)
    lo, hi = lo - 2, hi + 2
    total = hi - lo

    def find_state(v):
        for g in range(CHUNKS):
            start, stop = edges(step, g)
            if v < stop:
                return g, -start, False
        return 0, -TILES - 2 * step, True

    def find_rate(v):
        if v < TILES:
            return chunk_of(v), -CUTS[chunk_of(v)], False
        return 0, -TILES, True

    def cell(sp, p, v, h, at):
        g, off, rolled = at
        source, plane = LINE[p]
        ref, q = state[g][source], 2 * sp + plane
        if g == 0 and step == FLAT:
            return moved(ref[(q * (CUTS[1] - 4 * step) + v + off) * 2 + h], rolled)
        return moved(ref[q, v + off, h], rolled)

    def put(q, i, h, x):
        if extra is None:
            out[q, i, h] = x
        else:
            out[(q * (total - 4) + i) * 2 + h] = x

    def coef(k, place, v, h, at):
        g, off, rolled = at
        return moved(rate[g][(2, 0, 1, 3)[place]][4 + k, v + off, h], rolled)

    def ahead(u, v, near_u, near_v, f, cv):
        uvv = u * v * v
        return DU * near_u + (1.0 - 6.0 * DU) * u + f * (1.0 - u) - uvv, DV * near_v + cv * v + uvv

    def first(v, key):
        below, here, above, at = key
        c = [[cell(sp, p, v, h, here) for h in range(2)] for sp in range(2) for p in range(6)]
        for p in range(1, 5):
            for h in range(2):
                near = []
                for sp in range(2):
                    i = 6 * sp + p
                    s = cell(sp, p, v - 1, h, below) + cell(sp, p, v + 1, h, above)
                    near.append(beside(c[i][1 - h], h) + (s + (c[i - 1][h] + c[i + 1][h])))
                nu, nv = ahead(c[p][h], c[6 + p][h], *near, coef(0, p - 1, v, h, at), coef(1, p - 1, v, h, at))
                mids[0, p - 1, v - lo, h] = nu
                mids[1, p - 1, v - lo, h] = nv

    def then(v, key):
        here, at = key
        c = [[mids[sp, p, v - lo, h] for h in range(2)] for sp in range(2) for p in range(4)]
        for p in range(1, 3):
            for h in range(2):
                near = []
                for sp in range(2):
                    i = 4 * sp + p
                    s = mids[sp, p, v - lo - 1, h] + mids[sp, p, v - lo + 1, h]
                    near.append(beside(c[i][1 - h], h) + (s + (c[i - 1][h] + c[i + 1][h])))
                nu, nv = ahead(c[p][h], c[4 + p][h], *near, coef(0, p, v, h, at), coef(1, p, v, h, at))
                put(p - 1, v - lo - 2, h, 0.5 * (cell(0, p + 1, v, h, here) + nu))
                put(2 + p - 1, v - lo - 2, h, 0.5 * (cell(1, p + 1, v, h, here) + nv))

    if extra is not None:
        for k in range(4):
            for j in range(16):
                out[TAIL + 16 * k + j] = extra[k, j]

    over(lo + 1, hi - 1, lambda v: (find_state(v - 1), find_state(v), find_state(v + 1), find_rate(v)), first)
    over(lo + 2, hi - 2, lambda v: (find_state(v), find_rate(v)), then)


def heun(step, c, state, rate, after, extra=None):
    lo, hi = edges(step + 1, c)
    ins = [r for g in state[:c + 1] for r in g] + [r for g in rate[:c + 1] for r in g]
    shape = (4, hi - lo, 2, 8, 128)
    if extra is not None:
        ins = [extra] + ins
        shape = (TAIL + 64, 8, 128)
    return pl.pallas_call(
        functools.partial(heun_kernel, step, c),
        out_shape=jax.ShapeDtypeStruct(shape, F32),
        in_specs=[ANY] + [VM] * len(ins),
        out_specs=VM,
        scratch_shapes=[pltpu.VMEM((2, 4, hi - lo + 4, 2, 8, 128), F32)],
        compiler_params=PARAMS,
        cost_estimate=pl.CostEstimate(flops=COST[c][step], bytes_accessed=1000, transcendentals=0),
        name="heun_%s%d" % ("abcd"[c], step),
    )(after, *ins)


def mean_tile(tiles):
    s = [tiles[i] + tiles[i + 1] for i in range(0, 8, 2)]
    return 0.125 * ((s[0] + s[1]) + (s[2] + s[3]))


def mean_of(chunks, j, rows):
    c = chunk_of(2 * j)
    return mean_tile([chunks[c][q, 2 * j + i - CUTS[c], h] for q in rows for i in range(2) for h in range(2)])


def euler(get, cf, ccv, j):
    new = []
    for sp in range(2):
        c = get(0, sp, j)
        up = get(0, sp, j + 1) if j < 15 else pltpu.roll(get(0, sp, 0), 7, 0)
        down = get(0, sp, j - 1) if j else pltpu.roll(get(0, sp, 15), 1, 0)
        s = pltpu.roll(c, 1, 1) + pltpu.roll(c, 127, 1) + (up + down)
        new.append((c, s + (get(-1, sp, j) + get(1, sp, j))))
    (u, su), (v, sv) = new
    uvv = u * v * v
    nu = u + 2.0 * (0.25 * DU * (su - 6.0 * u) - uvv + cf * (1.0 - u))
    nv = v + 2.0 * (0.25 * DV * (sv - 6.0 * v) + uvv - ccv * v)
    return nu, nv


def own_first_kernel(*refs):
    pair, cross, got_pair, got_cross = [refs[CHUNKS * i:CHUNKS * (i + 1)] for i in range(4)]
    out, line = refs[4 * CHUNKS:]
    for j in range(16):
        for sp in range(2):
            rows = (2 * sp, 2 * sp + 1)
            line[0, sp, j] = mean_of(got_cross, j, rows)
            line[1, sp, j] = mean_of(pair, j, rows)
            line[2, sp, j] = mean_of(got_pair, j, rows)
        for k in range(2):
            c = chunk_of(2 * j)
            m = mean_tile([r[c][4 + k, 2 * j + i - CUTS[c], h] for r in (cross, pair) for i in range(2) for h in range(2)])
            out[2 + k, j] = m if k == 0 else 0.52 - m
    for j in range(16):
        out[0, j], out[1, j] = euler(lambda d, sp, i: line[1 + d, sp, i], out[2, j], out[3, j], j)


def own_first(*refs):
    return pl.pallas_call(
        own_first_kernel,
        out_shape=jax.ShapeDtypeStruct((4, 16, 8, 128), F32),
        in_specs=[VM] * (4 * CHUNKS),
        out_specs=VM,
        scratch_shapes=[pltpu.VMEM((3,) + COARSE, F32)],
        compiler_params=PARAMS,
        name="own_first",
    )(*refs)


def fine_tile(ends, q, v, h):
    rolled = v < 2 * FSTEPS
    v = v + TILES if rolled else v
    c = min(c for c in range(CHUNKS) if v < edges(FSTEPS, c)[1])
    x = ends[c][q, v - edges(FSTEPS, c)[0], h]
    return pltpu.roll(x, 1, 0) if rolled else x


def tails_kernel(after, cross, pair, cross_rate, pair_rate):
    for k in range(2):
        for j in range(16):
            cross_rate[k, j] = cross[TAIL + 16 * (2 + k) + j]
            pair_rate[k, j] = pair[TAIL + 16 * (2 + k) + j]


def tails(cross, pair, after):
    shape = jax.ShapeDtypeStruct(COARSE, F32)
    return pl.pallas_call(
        tails_kernel,
        out_shape=[shape] * 2,
        in_specs=[ANY, VM, VM],
        out_specs=[VM] * 2,
        compiler_params=PARAMS,
        name="tails",
    )(after, cross, pair)


def jump_kernel(here, cross, pair, *refs):
    ends, (end, send) = refs[:CHUNKS], refs[CHUNKS:]
    first = lax.axis_index("tm") == 0

    def get(d, sp, j):
        return here[sp, j] if d == 0 else (cross if d < 0 else pair)[TAIL + 16 * sp + j]

    for j in range(16):
        g = euler(get, here[2, j], here[3, j], j)
        for sp in range(2):
            m = mean_tile([fine_tile(ends, 2 * sp + q, 2 * j + i, h) for q in range(2) for i in range(2) for h in range(2)])
            end[sp, j] = m
            jump = m - g[sp]
            send[sp, j] = jnp.where(first, g[sp] + jump, jump)


def jump_of(ends, here, cross, pair):
    shape = jax.ShapeDtypeStruct(COARSE, F32)
    return pl.pallas_call(
        jump_kernel,
        out_shape=[shape] * 2,
        in_specs=[VM] * (3 + CHUNKS),
        out_specs=[VM] * 2,
        compiler_params=PARAMS,
        name="jump",
    )(here, cross, pair, *ends)


def pack_kernel(after, one, other, out):
    out[0] = one[...]
    out[1] = other[...]


def pack(one, other, after, flops=1000):
    return pl.pallas_call(
        pack_kernel,
        out_shape=jax.ShapeDtypeStruct((2,) + COARSE, F32),
        in_specs=[ANY, VM, VM],
        out_specs=VM,
        compiler_params=PARAMS,
        cost_estimate=pl.CostEstimate(flops=flops, bytes_accessed=1000, transcendentals=0),
        name="pack",
    )(after, one, other)


def walk_kernel(least, both, near, far, q_own, r_cross, r_pair, r_far, jumps, out, mid):
    line = ((near, 1), (near, 0), (both, 0), (both, 1), (far, 0), (far, 1))
    rates = ((r_cross, 0), (q_own, 2), (r_pair, 0), (r_far, 0))
    counts = lax.axis_index("tm") >= least
    for p in range(1, 5):
        q, k = rates[p - 1]
        for j in range(16):
            new = euler(lambda d, sp, i: line[p + d][0][line[p + d][1], sp, i], q[k, j], q[k + 1, j], j)
            mid[p - 1, 0, j], mid[p - 1, 1, j] = new
    single = len(jumps.shape) == 3 + 1
    for n in range(1 if single else 2):
        q, k = rates[n + 1]
        for j in range(16):
            new = euler(lambda d, sp, i: mid[n + 1 + d, sp, i], q[k, j], q[k + 1, j], j)
            for sp in range(2):
                x = jnp.where(counts, new[sp], 0.0)
                if single:
                    out[sp, j] = x + jumps[sp, j]
                else:
                    out[n, sp, j] = x + jumps[n, sp, j]


def walk(least, both, near, far, rates, jumps):
    return pl.pallas_call(
        functools.partial(walk_kernel, least),
        out_shape=jax.ShapeDtypeStruct(jumps.shape, F32),
        in_specs=[VM] * 8,
        out_specs=VM,
        scratch_shapes=[pltpu.VMEM((4,) + COARSE, F32)],
        compiler_params=PARAMS,
        name="walk%d" % least,
    )(both, near, far, *rates, jumps)


def finish_kernel(end, chained, *refs):
    ends, (out, rows, done, sems) = refs[:CHUNKS], refs[CHUNKS:]
    mat = splitter(True)
    flip = odd()
    copies = []
    for sp in range(2):
        shift = [chained[sp, j] - end[sp, j] for j in range(16)]
        for q in range(2):
            k = 2 * sp + q
            for v in range(TILES):
                for h in range(2):
                    rows[k, h, pl.ds(v, 8, stride=STRIDE), :] = fine_tile(ends, k, v, h) + shift[v // 2]
            halves = [jnp.concatenate([rows[k, h, pl.ds(STRIDE * band, TILES), :] for band in range(8)], axis=0) for h in range(2)]
            done[k] = permuted(jnp.concatenate(halves, axis=1), mat)
            copies.append(pltpu.make_async_copy(done.at[k], out.at[sp, q ^ flip], sems.at[k]))
            copies[-1].start()
    for c in copies:
        c.wait()


def finish(ends, end, chained):
    return pl.pallas_call(
        finish_kernel,
        out_shape=jax.ShapeDtypeStruct((2, 2, 256, 256), F32),
        in_specs=[VM] * (2 + CHUNKS),
        out_specs=pl.BlockSpec(memory_space=pltpu.HBM),
        scratch_shapes=[
            pltpu.VMEM((4, 2, 8 * STRIDE, 128), F32),
            pltpu.VMEM((4, 256, 256), F32),
            pltpu.SemaphoreType.DMA((4,)),
        ],
        compiler_params=PARAMS,
        name="finish",
    )(end, chained, *ends)


def swap_pair(x):
    n = lax.axis_size("space")
    return lax.ppermute(x, "space", [(i, i ^ 1) for i in range(n)])


def swap_cross(x):
    n = lax.axis_size("space")
    return lax.ppermute(x, "space", [(i, (i + 1) % n if i % 2 else (i - 1) % n) for i in range(n)])


def later(x, distance):
    n = lax.axis_size("tm")
    return lax.ppermute(x, "tm", [(i, i + distance) for i in range(n - distance)])


def body(slice_starts, feed, kill):
    sent = prep(slice_starts[0], feed, kill)
    pair, cross = sent[:CHUNKS], sent[CHUNKS:]
    got = [(swap_pair(p), swap_cross(c)) for p, c in zip(pair, cross)]
    got_pair, got_cross = [g[0] for g in got], [g[1] for g in got]
    rate = list(zip(cross, pair, got_cross, got_pair))
    state = list(zip(pair, got_cross, got_pair))
    own = own_first(*pair, *cross, *got_pair, *got_cross)
    before = pair[0]
    for step in range(FSTEPS):
        last = step == FSTEPS - 1
        made = []
        for c in range(CHUNKS):
            if last and c == CHUNKS - 1:
                tail = state[0][1:]
                rate_cross, rate_pair = tails(*tail, before)
                before = rate_far = swap_pair(rate_cross)
            new = heun(step, c, state, rate, before, own if step == FLAT - 1 and c == 0 else None)
            before = new
            made.append((new,) if last else (new, swap_cross(new), swap_pair(new)))
        state = made
    ends = [m[0] for m in state]
    end, send = jump_of(ends, own, *tail)
    rates = (own, rate_cross, rate_pair, rate_far)
    from3, from2, from1 = later(send, 3), later(send, 2), later(send, 1)
    both = pack(from3, swap_pair(from3), rate_far)
    jumps2 = pack(from2, swap_pair(from2), rate_far, PACK_COST)
    jumps1 = pack(from1, swap_pair(from1), rate_far, PACK_COST)
    for least, jumps in ((3, jumps2), (2, jumps1), (1, send)):
        near = swap_cross(both)
        far = swap_pair(near)
        both = walk(least, both, near, far, rates, jumps)
    return finish(ends, end, both)[None]


def solution(mesh):
    in_specs = (P("tm", None, "space", None, None), P("space", None, None), P("space", None, None))
    out_specs = P("tm", None, "space", None, None)
    return jax.shard_map(body, mesh=mesh, in_specs=in_specs, out_specs=out_specs, check_vma=False)
```

```python
import functools

import jax
import jax.numpy as jnp
from jax import lax
from jax.experimental import pallas as pl
from jax.experimental.pallas import tpu as pltpu
from jax.sharding import PartitionSpec as P

FSTEPS = 4
CSTEPS = 2
DU = 0.16
DV = 0.08
CUTS = (0, 18, 26, 32)
TILES = 32
STRIDE = 33
CHUNKS = len(CUTS) - 1
F32 = jnp.float32
UNROLL = 8
VMEM_LIMIT = 16 * 1024 * 1024

VM = pl.BlockSpec(memory_space=pltpu.VMEM)
ANY = pl.BlockSpec(memory_space=pl.ANY)
PARAMS = pltpu.CompilerParams(vmem_limit_bytes=VMEM_LIMIT)
COARSE = (2, 16, 8, 128)
PACK_COST = 10**10
RATES_COST = 2 * 10**9
COST = ((2 * 10**9,) * 4, (2 * 10**9,) * 2 + (4 * 10**9,) * 2, (2 * 10**9,) * 4)
FLAT = 3
TAIL = 4 * (CUTS[1] - 4 * FLAT) * 2


def splitter(transposed):
    r = lax.broadcasted_iota(jnp.int32, (256, 256), 0)
    c = lax.broadcasted_iota(jnp.int32, (256, 256), 1)
    if transposed:
        r, c = c, r
    return jnp.where(r == 2 * (c % 128) + c // 128, 1.0, 0.0).astype(jnp.bfloat16)


def permuted(x, mat):
    high = x.astype(jnp.bfloat16)
    rest = x - high.astype(F32)
    mid = rest.astype(jnp.bfloat16)
    low = (rest - mid.astype(F32)).astype(jnp.bfloat16)
    dot = lambda p: jnp.dot(p, mat, preferred_element_type=F32)
    return dot(high) + (dot(mid) + dot(low))


def odd():
    return lax.rem(lax.axis_index("space"), 2)


def chunk_of(v):
    return max(c for c in range(CHUNKS) if CUTS[c] <= v)


def scatter(plane, rows, mat, targets):
    done = permuted(plane, mat)
    for band in range(8):
        for h in range(2):
            rows[h, pl.ds(STRIDE * band, TILES), :] = done[TILES * band:TILES * (band + 1), 128 * h:128 * (h + 1)]
    for i in range(TILES):
        c = chunk_of(i)
        for h in range(2):
            tile = rows[h, pl.ds(i, 8, stride=STRIDE), :]
            for refs, q in targets:
                refs[c][q, i - CUTS[c], h] = tile


def prep_kernel(x, *refs):
    pair, cross, rows = refs[:CHUNKS], refs[CHUNKS:2 * CHUNKS], refs[-1]
    flip = odd()
    mat = splitter(False)
    for sp in range(2):
        for q in range(2):
            k = 2 * sp + q
            scatter(x[sp, q ^ flip], rows.at[k], mat, [(pair, k), (cross, k)])


def prep_rates_kernel(q, feed, kill, *refs):
    target, rows = refs[CHUNKS:2 * CHUNKS], refs[-1]
    flip = odd()
    mat = splitter(False)
    f = feed[q ^ flip]
    scatter(f, rows.at[0], mat, [(target, 4)])
    scatter(0.52 - (f + kill[q ^ flip]), rows.at[1], mat, [(target, 5)])


def prep(x, feed, kill):
    shapes = [jax.ShapeDtypeStruct((6, CUTS[c + 1] - CUTS[c], 2, 8, 128), F32) for c in range(CHUNKS)] * 2
    scratch = [pltpu.VMEM((4, 2, 8 * STRIDE, 128), F32)]
    sent = pl.pallas_call(
        prep_kernel,
        out_shape=shapes,
        in_specs=[VM],
        out_specs=[VM] * (2 * CHUNKS),
        scratch_shapes=scratch,
        compiler_params=PARAMS,
        name="prep",
    )(x)
    rated = []
    for q, part in ((0, sent[CHUNKS:]), (1, sent[:CHUNKS])):
        rated.append(pl.pallas_call(
            functools.partial(prep_rates_kernel, q),
            out_shape=shapes[:CHUNKS],
            in_specs=[VM] * (2 + CHUNKS),
            out_specs=[VM] * CHUNKS,
            scratch_shapes=[pltpu.VMEM((2, 2, 8 * STRIDE, 128), F32)],
            input_output_aliases={2 + c: c for c in range(CHUNKS)},
            compiler_params=PARAMS,
            cost_estimate=pl.CostEstimate(flops=RATES_COST, bytes_accessed=1000, transcendentals=0),
            name="prep_inner" if q else "prep_outer",
        )(feed, kill, *part))
    return rated[1] + rated[0]


LINE = ((1, 1), (1, 0), (0, 0), (0, 1), (2, 1), (2, 0))


def runs(lo, hi, key):
    out = []
    for v in range(lo, hi):
        k = key(v)
        if out and out[-1][2] == k:
            out[-1][1] = v + 1
        else:
            out.append([v, v + 1, k])
    return out


def over(lo, hi, key, work):
    for start, stop, k in runs(lo, hi, key):
        if stop - start < 4:
            for v in range(start, stop):
                work(v, k)
        else:
            @pl.loop(start, stop, unroll=min(UNROLL, stop - start))
            def _(v):
                work(v, k)


def moved(x, rolled):
    return pltpu.roll(x, 7, 0) if rolled else x


def beside(other, h):
    return other + pltpu.roll(other, 1 if h == 0 else 127, 1)


def edges(step, c):
    lo = CUTS[c] + (2 * step if c == 0 else -2 * step)
    return lo, CUTS[c + 1] + (2 * step if c == CHUNKS - 1 else -2 * step)


def heun_kernel(step, c, after, *refs):
    refs = list(refs)
    extra = refs.pop(0) if step == FLAT - 1 and c == 0 else None
    state = [refs[3 * g:3 * g + 3] for g in range(c + 1)]
    refs = refs[3 * (c + 1):]
    rate = [refs[4 * g:4 * g + 4] for g in range(c + 1)]
    out, mids = refs[-2:]
    lo, hi = edges(step + 1, c)
    lo, hi = lo - 2, hi + 2
    total = hi - lo

    def find_state(v):
        for g in range(CHUNKS):
            start, stop = edges(step, g)
            if v < stop:
                return g, -start, False
        return 0, -TILES - 2 * step, True

    def find_rate(v):
        if v < TILES:
            return chunk_of(v), -CUTS[chunk_of(v)], False
        return 0, -TILES, True

    def cell(sp, p, v, h, at):
        g, off, rolled = at
        source, plane = LINE[p]
        ref, q = state[g][source], 2 * sp + plane
        if g == 0 and step == FLAT:
            return moved(ref[(q * (CUTS[1] - 4 * step) + v + off) * 2 + h], rolled)
        return moved(ref[q, v + off, h], rolled)

    def put(q, i, h, x):
        if extra is None:
            out[q, i, h] = x
        else:
            out[(q * (total - 4) + i) * 2 + h] = x

    def coef(k, place, v, h, at):
        g, off, rolled = at
        return moved(rate[g][(2, 0, 1, 3)[place]][4 + k, v + off, h], rolled)

    def ahead(u, v, near_u, near_v, f, cv):
        uvv = u * v * v
        return DU * near_u + (1.0 - 6.0 * DU) * u + f * (1.0 - u) - uvv, DV * near_v + cv * v + uvv

    def first(v, key):
        below, here, above, at = key
        c = [[cell(sp, p, v, h, here) for h in range(2)] for sp in range(2) for p in range(6)]
        for p in range(1, 5):
            for h in range(2):
                near = []
                for sp in range(2):
                    i = 6 * sp + p
                    s = cell(sp, p, v - 1, h, below) + cell(sp, p, v + 1, h, above)
                    near.append(beside(c[i][1 - h], h) + (s + (c[i - 1][h] + c[i + 1][h])))
                nu, nv = ahead(c[p][h], c[6 + p][h], *near, coef(0, p - 1, v, h, at), coef(1, p - 1, v, h, at))
                mids[0, p - 1, v - lo, h] = nu
                mids[1, p - 1, v - lo, h] = nv

    def then(v, key):
        here, at = key
        c = [[mids[sp, p, v - lo, h] for h in range(2)] for sp in range(2) for p in range(4)]
        for p in range(1, 3):
            for h in range(2):
                near = []
                for sp in range(2):
                    i = 4 * sp + p
                    s = mids[sp, p, v - lo - 1, h] + mids[sp, p, v - lo + 1, h]
                    near.append(beside(c[i][1 - h], h) + (s + (c[i - 1][h] + c[i + 1][h])))
                nu, nv = ahead(c[p][h], c[4 + p][h], *near, coef(0, p, v, h, at), coef(1, p, v, h, at))
                put(p - 1, v - lo - 2, h, 0.5 * (cell(0, p + 1, v, h, here) + nu))
                put(2 + p - 1, v - lo - 2, h, 0.5 * (cell(1, p + 1, v, h, here) + nv))

    if extra is not None:
        for k in range(4):
            for j in range(16):
                out[TAIL + 16 * k + j] = extra[k, j]

    over(lo + 1, hi - 1, lambda v: (find_state(v - 1), find_state(v), find_state(v + 1), find_rate(v)), first)
    over(lo + 2, hi - 2, lambda v: (find_state(v), find_rate(v)), then)


def heun(step, c, state, rate, after, extra=None):
    lo, hi = edges(step + 1, c)
    ins = [r for g in state[:c + 1] for r in g] + [r for g in rate[:c + 1] for r in g]
    shape = (4, hi - lo, 2, 8, 128)
    if extra is not None:
        ins = [extra] + ins
        shape = (TAIL + 64, 8, 128)
    return pl.pallas_call(
        functools.partial(heun_kernel, step, c),
        out_shape=jax.ShapeDtypeStruct(shape, F32),
        in_specs=[ANY] + [VM] * len(ins),
        out_specs=VM,
        scratch_shapes=[pltpu.VMEM((2, 4, hi - lo + 4, 2, 8, 128), F32)],
        compiler_params=PARAMS,
        cost_estimate=pl.CostEstimate(flops=COST[c][step], bytes_accessed=1000, transcendentals=0),
        name="heun_%s%d" % ("abcd"[c], step),
    )(after, *ins)


def mean_tile(tiles):
    s = [tiles[i] + tiles[i + 1] for i in range(0, 8, 2)]
    return 0.125 * ((s[0] + s[1]) + (s[2] + s[3]))


def mean_of(chunks, j, rows):
    c = chunk_of(2 * j)
    return mean_tile([chunks[c][q, 2 * j + i - CUTS[c], h] for q in rows for i in range(2) for h in range(2)])


def euler(get, cf, ccv, j):
    new = []
    for sp in range(2):
        c = get(0, sp, j)
        up = get(0, sp, j + 1) if j < 15 else pltpu.roll(get(0, sp, 0), 7, 0)
        down = get(0, sp, j - 1) if j else pltpu.roll(get(0, sp, 15), 1, 0)
        s = pltpu.roll(c, 1, 1) + pltpu.roll(c, 127, 1) + (up + down)
        new.append((c, s + (get(-1, sp, j) + get(1, sp, j))))
    (u, su), (v, sv) = new
    uvv = u * v * v
    nu = u + 2.0 * (0.25 * DU * (su - 6.0 * u) - uvv + cf * (1.0 - u))
    nv = v + 2.0 * (0.25 * DV * (sv - 6.0 * v) + uvv - ccv * v)
    return nu, nv


def own_first_kernel(*refs):
    pair, cross, got_pair, got_cross = [refs[CHUNKS * i:CHUNKS * (i + 1)] for i in range(4)]
    out, line = refs[4 * CHUNKS:]
    for j in range(16):
        for sp in range(2):
            rows = (2 * sp, 2 * sp + 1)
            line[0, sp, j] = mean_of(got_cross, j, rows)
            line[1, sp, j] = mean_of(pair, j, rows)
            line[2, sp, j] = mean_of(got_pair, j, rows)
        for k in range(2):
            c = chunk_of(2 * j)
            m = mean_tile([r[c][4 + k, 2 * j + i - CUTS[c], h] for r in (cross, pair) for i in range(2) for h in range(2)])
            out[2 + k, j] = m if k == 0 else 0.52 - m
    for j in range(16):
        out[0, j], out[1, j] = euler(lambda d, sp, i: line[1 + d, sp, i], out[2, j], out[3, j], j)


def own_first(*refs):
    return pl.pallas_call(
        own_first_kernel,
        out_shape=jax.ShapeDtypeStruct((4, 16, 8, 128), F32),
        in_specs=[VM] * (4 * CHUNKS),
        out_specs=VM,
        scratch_shapes=[pltpu.VMEM((3,) + COARSE, F32)],
        compiler_params=PARAMS,
        name="own_first",
    )(*refs)


def fine_tile(ends, q, v, h):
    rolled = v < 2 * FSTEPS
    v = v + TILES if rolled else v
    c = min(c for c in range(CHUNKS) if v < edges(FSTEPS, c)[1])
    x = ends[c][q, v - edges(FSTEPS, c)[0], h]
    return pltpu.roll(x, 1, 0) if rolled else x


def tails_kernel(after, cross, pair, cross_rate, pair_rate):
    for k in range(2):
        for j in range(16):
            cross_rate[k, j] = cross[TAIL + 16 * (2 + k) + j]
            pair_rate[k, j] = pair[TAIL + 16 * (2 + k) + j]


def tails(cross, pair, after):
    shape = jax.ShapeDtypeStruct(COARSE, F32)
    return pl.pallas_call(
        tails_kernel,
        out_shape=[shape] * 2,
        in_specs=[ANY, VM, VM],
        out_specs=[VM] * 2,
        compiler_params=PARAMS,
        name="tails",
    )(after, cross, pair)


def jump_kernel(here, cross, pair, *refs):
    ends, (end, send) = refs[:CHUNKS], refs[CHUNKS:]
    first = lax.axis_index("tm") == 0

    def get(d, sp, j):
        return here[sp, j] if d == 0 else (cross if d < 0 else pair)[TAIL + 16 * sp + j]

    for j in range(16):
        g = euler(get, here[2, j], here[3, j], j)
        for sp in range(2):
            m = mean_tile([fine_tile(ends, 2 * sp + q, 2 * j + i, h) for q in range(2) for i in range(2) for h in range(2)])
            end[sp, j] = m
            jump = m - g[sp]
            send[sp, j] = jnp.where(first, g[sp] + jump, jump)


def jump_of(ends, here, cross, pair):
    shape = jax.ShapeDtypeStruct(COARSE, F32)
    return pl.pallas_call(
        jump_kernel,
        out_shape=[shape] * 2,
        in_specs=[VM] * (3 + CHUNKS),
        out_specs=[VM] * 2,
        compiler_params=PARAMS,
        name="jump",
    )(here, cross, pair, *ends)


def pack_kernel(after, one, other, out):
    out[0] = one[...]
    out[1] = other[...]


def pack(one, other, after, flops=1000):
    return pl.pallas_call(
        pack_kernel,
        out_shape=jax.ShapeDtypeStruct((2,) + COARSE, F32),
        in_specs=[ANY, VM, VM],
        out_specs=VM,
        compiler_params=PARAMS,
        cost_estimate=pl.CostEstimate(flops=flops, bytes_accessed=1000, transcendentals=0),
        name="pack",
    )(after, one, other)


def walk_kernel(least, both, near, far, q_own, r_cross, r_pair, r_far, jumps, out, mid):
    line = ((near, 1), (near, 0), (both, 0), (both, 1), (far, 0), (far, 1))
    rates = ((r_cross, 0), (q_own, 2), (r_pair, 0), (r_far, 0))
    counts = lax.axis_index("tm") >= least
    for p in range(1, 5):
        q, k = rates[p - 1]
        for j in range(16):
            new = euler(lambda d, sp, i: line[p + d][0][line[p + d][1], sp, i], q[k, j], q[k + 1, j], j)
            mid[p - 1, 0, j], mid[p - 1, 1, j] = new
    single = len(jumps.shape) == 3 + 1
    for n in range(1 if single else 2):
        q, k = rates[n + 1]
        for j in range(16):
            new = euler(lambda d, sp, i: mid[n + 1 + d, sp, i], q[k, j], q[k + 1, j], j)
            for sp in range(2):
                x = jnp.where(counts, new[sp], 0.0)
                if single:
                    out[sp, j] = x + jumps[sp, j]
                else:
                    out[n, sp, j] = x + jumps[n, sp, j]


def walk(least, both, near, far, rates, jumps):
    return pl.pallas_call(
        functools.partial(walk_kernel, least),
        out_shape=jax.ShapeDtypeStruct(jumps.shape, F32),
        in_specs=[VM] * 8,
        out_specs=VM,
        scratch_shapes=[pltpu.VMEM((4,) + COARSE, F32)],
        compiler_params=PARAMS,
        name="walk%d" % least,
    )(both, near, far, *rates, jumps)


def finish_kernel(end, chained, *refs):
    ends, (out, rows, done, sems) = refs[:CHUNKS], refs[CHUNKS:]
    mat = splitter(True)
    flip = odd()
    copies = []
    for sp in range(2):
        shift = [chained[sp, j] - end[sp, j] for j in range(16)]
        for q in range(2):
            k = 2 * sp + q
            for v in range(TILES):
                for h in range(2):
                    rows[k, h, pl.ds(v, 8, stride=STRIDE), :] = fine_tile(ends, k, v, h) + shift[v // 2]
            halves = [jnp.concatenate([rows[k, h, pl.ds(STRIDE * band, TILES), :] for band in range(8)], axis=0) for h in range(2)]
            done[k] = permuted(jnp.concatenate(halves, axis=1), mat)
            copies.append(pltpu.make_async_copy(done.at[k], out.at[sp, q ^ flip], sems.at[k]))
            copies[-1].start()
    for c in copies:
        c.wait()


def finish(ends, end, chained):
    return pl.pallas_call(
        finish_kernel,
        out_shape=jax.ShapeDtypeStruct((2, 2, 256, 256), F32),
        in_specs=[VM] * (2 + CHUNKS),
        out_specs=pl.BlockSpec(memory_space=pltpu.HBM),
        scratch_shapes=[
            pltpu.VMEM((4, 2, 8 * STRIDE, 128), F32),
            pltpu.VMEM((4, 256, 256), F32),
            pltpu.SemaphoreType.DMA((4,)),
        ],
        compiler_params=PARAMS,
        name="finish",
    )(end, chained, *ends)


def swap_pair(x):
    n = lax.axis_size("space")
    return lax.ppermute(x, "space", [(i, i ^ 1) for i in range(n)])


def swap_cross(x):
    n = lax.axis_size("space")
    return lax.ppermute(x, "space", [(i, (i + 1) % n if i % 2 else (i - 1) % n) for i in range(n)])


def later(x, distance):
    n = lax.axis_size("tm")
    return lax.ppermute(x, "tm", [(i, i + distance) for i in range(n - distance)])


def body(slice_starts, feed, kill):
    sent = prep(slice_starts[0], feed, kill)
    pair, cross = sent[:CHUNKS], sent[CHUNKS:]
    got = [(swap_pair(p), swap_cross(c)) for p, c in zip(pair, cross)]
    got_pair, got_cross = [g[0] for g in got], [g[1] for g in got]
    rate = list(zip(cross, pair, got_cross, got_pair))
    state = list(zip(pair, got_cross, got_pair))
    own = own_first(*pair, *cross, *got_pair, *got_cross)
    before = pair[0]
    for step in range(FSTEPS):
        last = step == FSTEPS - 1
        made = []
        for c in range(CHUNKS):
            if last and c == CHUNKS - 1:
                tail = state[0][1:]
                rate_cross, rate_pair = tails(*tail, before)
                before = rate_far = swap_pair(rate_cross)
            new = heun(step, c, state, rate, before, own if step == FLAT - 1 and c == 0 else None)
            before = new
            made.append((new,) if last else (new, swap_cross(new), swap_pair(new)))
        state = made
    ends = [m[0] for m in state]
    end, send = jump_of(ends, own, *tail)
    rates = (own, rate_cross, rate_pair, rate_far)
    from3, from2, from1 = later(send, 3), later(send, 2), later(send, 1)
    both = pack(from3, swap_pair(from3), rate_far)
    jumps2 = pack(from2, swap_pair(from2), rate_far, PACK_COST)
    jumps1 = pack(from1, swap_pair(from1), rate_far, PACK_COST)
    for least, jumps in ((3, jumps2), (2, jumps1), (1, send)):
        near = swap_cross(both)
        far = swap_pair(near)
        both = walk(least, both, near, far, rates, jumps)
    return finish(ends, end, both)[None]


def solution(mesh):
    in_specs = (P("tm", None, "space", None, None), P("space", None, None), P("space", None, None))
    out_specs = P("tm", None, "space", None, None)
    return jax.shard_map(body, mesh=mesh, in_specs=in_specs, out_specs=out_specs, check_vma=False)
```

```python
import functools

import jax
import jax.numpy as jnp
from jax import lax
from jax.experimental import pallas as pl
from jax.experimental.pallas import tpu as pltpu
from jax.sharding import PartitionSpec as P

FSTEPS = 4
CSTEPS = 2
DU = 0.16
DV = 0.08
CUTS = (0, 18, 26, 32)
TILES = 32
STRIDE = 33
CHUNKS = len(CUTS) - 1
F32 = jnp.float32
UNROLL = 8
VMEM_LIMIT = 16 * 1024 * 1024

VM = pl.BlockSpec(memory_space=pltpu.VMEM)
ANY = pl.BlockSpec(memory_space=pl.ANY)
PARAMS = pltpu.CompilerParams(vmem_limit_bytes=VMEM_LIMIT)
COARSE = (2, 16, 8, 128)
PACK_COST = 10**10
RATES_COST = 2 * 10**9
COST = ((2 * 10**9,) * 4, (2 * 10**9,) * 2 + (4 * 10**9,) * 2, (2 * 10**9,) * 4)
FLAT = 3
TAIL = 4 * (CUTS[1] - 4 * FLAT) * 2


def splitter(transposed):
    r = lax.broadcasted_iota(jnp.int32, (256, 256), 0)
    c = lax.broadcasted_iota(jnp.int32, (256, 256), 1)
    if transposed:
        r, c = c, r
    return jnp.where(r == 2 * (c % 128) + c // 128, 1.0, 0.0).astype(jnp.bfloat16)


def permuted(x, mat):
    high = x.astype(jnp.bfloat16)
    rest = x - high.astype(F32)
    mid = rest.astype(jnp.bfloat16)
    low = (rest - mid.astype(F32)).astype(jnp.bfloat16)
    dot = lambda p: jnp.dot(p, mat, preferred_element_type=F32)
    return dot(high) + (dot(mid) + dot(low))


def odd():
    return lax.rem(lax.axis_index("space"), 2)


def chunk_of(v):
    return max(c for c in range(CHUNKS) if CUTS[c] <= v)


def scatter(plane, rows, mat, targets):
    done = permuted(plane, mat)
    for band in range(8):
        for h in range(2):
            rows[h, pl.ds(STRIDE * band, TILES), :] = done[TILES * band:TILES * (band + 1), 128 * h:128 * (h + 1)]
    for i in range(TILES):
        c = chunk_of(i)
        for h in range(2):
            tile = rows[h, pl.ds(i, 8, stride=STRIDE), :]
            for refs, q in targets:
                refs[c][q, i - CUTS[c], h] = tile


def prep_kernel(x, *refs):
    pair, cross, rows = refs[:CHUNKS], refs[CHUNKS:2 * CHUNKS], refs[-1]
    flip = odd()
    mat = splitter(False)
    for sp in range(2):
        for q in range(2):
            k = 2 * sp + q
            scatter(x[sp, q ^ flip], rows.at[k], mat, [(pair, k), (cross, k)])


def prep_rates_kernel(q, feed, kill, *refs):
    target, rows = refs[CHUNKS:2 * CHUNKS], refs[-1]
    flip = odd()
    mat = splitter(False)
    f = feed[q ^ flip]
    scatter(f, rows.at[0], mat, [(target, 4)])
    scatter(0.52 - (f + kill[q ^ flip]), rows.at[1], mat, [(target, 5)])


def prep(x, feed, kill):
    shapes = [jax.ShapeDtypeStruct((6, CUTS[c + 1] - CUTS[c], 2, 8, 128), F32) for c in range(CHUNKS)] * 2
    scratch = [pltpu.VMEM((4, 2, 9 * STRIDE, 128), F32)]
    sent = pl.pallas_call(
        prep_kernel,
        out_shape=shapes,
        in_specs=[VM],
        out_specs=[VM] * (2 * CHUNKS),
        scratch_shapes=scratch,
        compiler_params=PARAMS,
        name="prep",
    )(x)
    rated = []
    for q, part in ((0, sent[CHUNKS:]), (1, sent[:CHUNKS])):
        rated.append(pl.pallas_call(
            functools.partial(prep_rates_kernel, q),
            out_shape=shapes[:CHUNKS],
            in_specs=[VM] * (2 + CHUNKS),
            out_specs=[VM] * CHUNKS,
            scratch_shapes=[pltpu.VMEM((2, 2, 9 * STRIDE, 128), F32)],
            input_output_aliases={2 + c: c for c in range(CHUNKS)},
            compiler_params=PARAMS,
            cost_estimate=pl.CostEstimate(flops=RATES_COST, bytes_accessed=1000, transcendentals=0),
            name="prep_inner" if q else "prep_outer",
        )(feed, kill, *part))
    return rated[1] + rated[0]


LINE = ((1, 1), (1, 0), (0, 0), (0, 1), (2, 1), (2, 0))


def runs(lo, hi, key):
    out = []
    for v in range(lo, hi):
        k = key(v)
        if out and out[-1][2] == k:
            out[-1][1] = v + 1
        else:
            out.append([v, v + 1, k])
    return out


def over(lo, hi, key, work):
    for start, stop, k in runs(lo, hi, key):
        if stop - start < 4:
            for v in range(start, stop):
                work(v, k)
        else:
            @pl.loop(start, stop, unroll=min(UNROLL, stop - start))
            def _(v):
                work(v, k)


def moved(x, rolled):
    return pltpu.roll(x, 7, 0) if rolled else x


def beside(other, h):
    return other + pltpu.roll(other, 1 if h == 0 else 127, 1)


def edges(step, c):
    lo = CUTS[c] + (2 * step if c == 0 else -2 * step)
    return lo, CUTS[c + 1] + (2 * step if c == CHUNKS - 1 else -2 * step)


def heun_kernel(step, c, after, *refs):
    refs = list(refs)
    extra = refs.pop(0) if step == FLAT - 1 and c == 0 else None
    state = [refs[3 * g:3 * g + 3] for g in range(c + 1)]
    refs = refs[3 * (c + 1):]
    rate = [refs[4 * g:4 * g + 4] for g in range(c + 1)]
    out, mids = refs[-2:]
    lo, hi = edges(step + 1, c)
    lo, hi = lo - 2, hi + 2
    total = hi - lo

    def find_state(v):
        for g in range(CHUNKS):
            start, stop = edges(step, g)
            if v < stop:
                return g, -start, False
        return 0, -TILES - 2 * step, True

    def find_rate(v):
        if v < TILES:
            return chunk_of(v), -CUTS[chunk_of(v)], False
        return 0, -TILES, True

    def cell(sp, p, v, h, at):
        g, off, rolled = at
        source, plane = LINE[p]
        ref, q = state[g][source], 2 * sp + plane
        if g == 0 and step == FLAT:
            return moved(ref[(q * (CUTS[1] - 4 * step) + v + off) * 2 + h], rolled)
        return moved(ref[q, v + off, h], rolled)

    def put(q, i, h, x):
        if extra is None:
            out[q, i, h] = x
        else:
            out[(q * (total - 4) + i) * 2 + h] = x

    def coef(k, place, v, h, at):
        g, off, rolled = at
        return moved(rate[g][(2, 0, 1, 3)[place]][4 + k, v + off, h], rolled)

    def ahead(u, v, near_u, near_v, f, cv):
        uvv = u * v * v
        return DU * near_u + (1.0 - 6.0 * DU) * u + f * (1.0 - u) - uvv, DV * near_v + cv * v + uvv

    def first(v, key):
        below, here, above, at = key
        c = [[cell(sp, p, v, h, here) for h in range(2)] for sp in range(2) for p in range(6)]
        for p in range(1, 5):
            for h in range(2):
                near = []
                for sp in range(2):
                    i = 6 * sp + p
                    s = cell(sp, p, v - 1, h, below) + cell(sp, p, v + 1, h, above)
                    near.append(beside(c[i][1 - h], h) + (s + (c[i - 1][h] + c[i + 1][h])))
                nu, nv = ahead(c[p][h], c[6 + p][h], *near, coef(0, p - 1, v, h, at), coef(1, p - 1, v, h, at))
                mids[0, p - 1, v - lo, h] = nu
                mids[1, p - 1, v - lo, h] = nv

    def then(v, key):
        here, at = key
        c = [[mids[sp, p, v - lo, h] for h in range(2)] for sp in range(2) for p in range(4)]
        for p in range(1, 3):
            for h in range(2):
                near = []
                for sp in range(2):
                    i = 4 * sp + p
                    s = mids[sp, p, v - lo - 1, h] + mids[sp, p, v - lo + 1, h]
                    near.append(beside(c[i][1 - h], h) + (s + (c[i - 1][h] + c[i + 1][h])))
                nu, nv = ahead(c[p][h], c[4 + p][h], *near, coef(0, p, v, h, at), coef(1, p, v, h, at))
                put(p - 1, v - lo - 2, h, 0.5 * (cell(0, p + 1, v, h, here) + nu))
                put(2 + p - 1, v - lo - 2, h, 0.5 * (cell(1, p + 1, v, h, here) + nv))

    if extra is not None:
        for k in range(4):
            for j in range(16):
                out[TAIL + 16 * k + j] = extra[k, j]

    over(lo + 1, hi - 1, lambda v: (find_state(v - 1), find_state(v), find_state(v + 1), find_rate(v)), first)
    over(lo + 2, hi - 2, lambda v: (find_state(v), find_rate(v)), then)


def heun(step, c, state, rate, after, extra=None):
    lo, hi = edges(step + 1, c)
    ins = [r for g in state[:c + 1] for r in g] + [r for g in rate[:c + 1] for r in g]
    shape = (4, hi - lo, 2, 8, 128)
    if extra is not None:
        ins = [extra] + ins
        shape = (TAIL + 64, 8, 128)
    return pl.pallas_call(
        functools.partial(heun_kernel, step, c),
        out_shape=jax.ShapeDtypeStruct(shape, F32),
        in_specs=[ANY] + [VM] * len(ins),
        out_specs=VM,
        scratch_shapes=[pltpu.VMEM((2, 4, hi - lo + 4, 2, 8, 128), F32)],
        compiler_params=PARAMS,
        cost_estimate=pl.CostEstimate(flops=COST[c][step], bytes_accessed=1000, transcendentals=0),
        name="heun_%s%d" % ("abcd"[c], step),
    )(after, *ins)


def mean_tile(tiles):
    s = [tiles[i] + tiles[i + 1] for i in range(0, 8, 2)]
    return 0.125 * ((s[0] + s[1]) + (s[2] + s[3]))


def mean_of(chunks, j, rows):
    c = chunk_of(2 * j)
    return mean_tile([chunks[c][q, 2 * j + i - CUTS[c], h] for q in rows for i in range(2) for h in range(2)])


def euler(get, cf, ccv, j):
    new = []
    for sp in range(2):
        c = get(0, sp, j)
        up = get(0, sp, j + 1) if j < 15 else pltpu.roll(get(0, sp, 0), 7, 0)
        down = get(0, sp, j - 1) if j else pltpu.roll(get(0, sp, 15), 1, 0)
        s = pltpu.roll(c, 1, 1) + pltpu.roll(c, 127, 1) + (up + down)
        new.append((c, s + (get(-1, sp, j) + get(1, sp, j))))
    (u, su), (v, sv) = new
    uvv = u * v * v
    nu = u + 2.0 * (0.25 * DU * (su - 6.0 * u) - uvv + cf * (1.0 - u))
    nv = v + 2.0 * (0.25 * DV * (sv - 6.0 * v) + uvv - ccv * v)
    return nu, nv


def own_first_kernel(*refs):
    pair, cross, got_pair, got_cross = [refs[CHUNKS * i:CHUNKS * (i + 1)] for i in range(4)]
    out, line = refs[4 * CHUNKS:]
    for j in range(16):
        for sp in range(2):
            rows = (2 * sp, 2 * sp + 1)
            line[0, sp, j] = mean_of(got_cross, j, rows)
            line[1, sp, j] = mean_of(pair, j, rows)
            line[2, sp, j] = mean_of(got_pair, j, rows)
        for k in range(2):
            c = chunk_of(2 * j)
            m = mean_tile([r[c][4 + k, 2 * j + i - CUTS[c], h] for r in (cross, pair) for i in range(2) for h in range(2)])
            out[2 + k, j] = m if k == 0 else 0.52 - m
    for j in range(16):
        out[0, j], out[1, j] = euler(lambda d, sp, i: line[1 + d, sp, i], out[2, j], out[3, j], j)


def own_first(*refs):
    return pl.pallas_call(
        own_first_kernel,
        out_shape=jax.ShapeDtypeStruct((4, 16, 8, 128), F32),
        in_specs=[VM] * (4 * CHUNKS),
        out_specs=VM,
        scratch_shapes=[pltpu.VMEM((3,) + COARSE, F32)],
        compiler_params=PARAMS,
        name="own_first",
    )(*refs)


def fine_tile(ends, q, v, h):
    rolled = v < 2 * FSTEPS
    v = v + TILES if rolled else v
    c = min(c for c in range(CHUNKS) if v < edges(FSTEPS, c)[1])
    x = ends[c][q, v - edges(FSTEPS, c)[0], h]
    return pltpu.roll(x, 1, 0) if rolled else x


def tails_kernel(after, cross, pair, cross_rate, pair_rate):
    for k in range(2):
        for j in range(16):
            cross_rate[k, j] = cross[TAIL + 16 * (2 + k) + j]
            pair_rate[k, j] = pair[TAIL + 16 * (2 + k) + j]


def tails(cross, pair, after):
    shape = jax.ShapeDtypeStruct(COARSE, F32)
    return pl.pallas_call(
        tails_kernel,
        out_shape=[shape] * 2,
        in_specs=[ANY, VM, VM],
        out_specs=[VM] * 2,
        compiler_params=PARAMS,
        name="tails",
    )(after, cross, pair)


def jump_kernel(here, cross, pair, *refs):
    ends, (end, send) = refs[:CHUNKS], refs[CHUNKS:]
    first = lax.axis_index("tm") == 0

    def get(d, sp, j):
        return here[sp, j] if d == 0 else (cross if d < 0 else pair)[TAIL + 16 * sp + j]

    for j in range(16):
        g = euler(get, here[2, j], here[3, j], j)
        for sp in range(2):
            m = mean_tile([fine_tile(ends, 2 * sp + q, 2 * j + i, h) for q in range(2) for i in range(2) for h in range(2)])
            end[sp, j] = m
            jump = m - g[sp]
            send[sp, j] = jnp.where(first, g[sp] + jump, jump)


def jump_of(ends, here, cross, pair):
    shape = jax.ShapeDtypeStruct(COARSE, F32)
    return pl.pallas_call(
        jump_kernel,
        out_shape=[shape] * 2,
        in_specs=[VM] * (3 + CHUNKS),
        out_specs=[VM] * 2,
        compiler_params=PARAMS,
        name="jump",
    )(here, cross, pair, *ends)


def pack_kernel(after, one, other, out):
    out[0] = one[...]
    out[1] = other[...]


def pack(one, other, after, flops=1000):
    return pl.pallas_call(
        pack_kernel,
        out_shape=jax.ShapeDtypeStruct((2,) + COARSE, F32),
        in_specs=[ANY, VM, VM],
        out_specs=VM,
        compiler_params=PARAMS,
        cost_estimate=pl.CostEstimate(flops=flops, bytes_accessed=1000, transcendentals=0),
        name="pack",
    )(after, one, other)


def walk_kernel(least, both, near, far, q_own, r_cross, r_pair, r_far, jumps, out, mid):
    line = ((near, 1), (near, 0), (both, 0), (both, 1), (far, 0), (far, 1))
    rates = ((r_cross, 0), (q_own, 2), (r_pair, 0), (r_far, 0))
    counts = lax.axis_index("tm") >= least
    for p in range(1, 5):
        q, k = rates[p - 1]
        for j in range(16):
            new = euler(lambda d, sp, i: line[p + d][0][line[p + d][1], sp, i], q[k, j], q[k + 1, j], j)
            mid[p - 1, 0, j], mid[p - 1, 1, j] = new
    single = len(jumps.shape) == 3 + 1
    for n in range(1 if single else 2):
        q, k = rates[n + 1]
        for j in range(16):
            new = euler(lambda d, sp, i: mid[n + 1 + d, sp, i], q[k, j], q[k + 1, j], j)
            for sp in range(2):
                x = jnp.where(counts, new[sp], 0.0)
                if single:
                    out[sp, j] = x + jumps[sp, j]
                else:
                    out[n, sp, j] = x + jumps[n, sp, j]


def walk(least, both, near, far, rates, jumps):
    return pl.pallas_call(
        functools.partial(walk_kernel, least),
        out_shape=jax.ShapeDtypeStruct(jumps.shape, F32),
        in_specs=[VM] * 8,
        out_specs=VM,
        scratch_shapes=[pltpu.VMEM((4,) + COARSE, F32)],
        compiler_params=PARAMS,
        name="walk%d" % least,
    )(both, near, far, *rates, jumps)


def finish_kernel(end, chained, *refs):
    ends, (out, rows, done, sems) = refs[:CHUNKS], refs[CHUNKS:]
    mat = splitter(True)
    flip = odd()
    copies = []
    for sp in range(2):
        shift = [chained[sp, j] - end[sp, j] for j in range(16)]
        for q in range(2):
            k = 2 * sp + q
            for v in range(TILES):
                for h in range(2):
                    rows[k, h, pl.ds(v, 8, stride=STRIDE), :] = fine_tile(ends, k, v, h) + shift[v // 2]
            halves = [jnp.concatenate([rows[k, h, pl.ds(STRIDE * band, TILES), :] for band in range(8)], axis=0) for h in range(2)]
            done[k] = permuted(jnp.concatenate(halves, axis=1), mat)
            copies.append(pltpu.make_async_copy(done.at[k], out.at[sp, q ^ flip], sems.at[k]))
            copies[-1].start()
    for c in copies:
        c.wait()


def finish(ends, end, chained):
    return pl.pallas_call(
        finish_kernel,
        out_shape=jax.ShapeDtypeStruct((2, 2, 256, 256), F32),
        in_specs=[VM] * (2 + CHUNKS),
        out_specs=pl.BlockSpec(memory_space=pltpu.HBM),
        scratch_shapes=[
            pltpu.VMEM((4, 2, 9 * STRIDE, 128), F32),
            pltpu.VMEM((4, 256, 256), F32),
            pltpu.SemaphoreType.DMA((4,)),
        ],
        compiler_params=PARAMS,
        name="finish",
    )(end, chained, *ends)


def swap_pair(x):
    n = lax.axis_size("space")
    return lax.ppermute(x, "space", [(i, i ^ 1) for i in range(n)])


def swap_cross(x):
    n = lax.axis_size("space")
    return lax.ppermute(x, "space", [(i, (i + 1) % n if i % 2 else (i - 1) % n) for i in range(n)])


def later(x, distance):
    n = lax.axis_size("tm")
    return lax.ppermute(x, "tm", [(i, i + distance) for i in range(n - distance)])


def body(slice_starts, feed, kill):
    sent = prep(slice_starts[0], feed, kill)
    pair, cross = sent[:CHUNKS], sent[CHUNKS:]
    got = [(swap_pair(p), swap_cross(c)) for p, c in zip(pair, cross)]
    got_pair, got_cross = [g[0] for g in got], [g[1] for g in got]
    rate = list(zip(cross, pair, got_cross, got_pair))
    state = list(zip(pair, got_cross, got_pair))
    own = own_first(*pair, *cross, *got_pair, *got_cross)
    before = pair[0]
    for step in range(FSTEPS):
        last = step == FSTEPS - 1
        made = []
        for c in range(CHUNKS):
            if last and c == CHUNKS - 1:
                tail = state[0][1:]
                rate_cross, rate_pair = tails(*tail, before)
                before = rate_far = swap_pair(rate_cross)
            new = heun(step, c, state, rate, before, own if step == FLAT - 1 and c == 0 else None)
            before = new
            made.append((new,) if last else (new, swap_cross(new), swap_pair(new)))
        state = made
    ends = [m[0] for m in state]
    end, send = jump_of(ends, own, *tail)
    rates = (own, rate_cross, rate_pair, rate_far)
    from3, from2, from1 = later(send, 3), later(send, 2), later(send, 1)
    both = pack(from3, swap_pair(from3), rate_far)
    jumps2 = pack(from2, swap_pair(from2), rate_far, PACK_COST)
    jumps1 = pack(from1, swap_pair(from1), rate_far, PACK_COST)
    for least, jumps in ((3, jumps2), (2, jumps1), (1, send)):
        near = swap_cross(both)
        far = swap_pair(near)
        both = walk(least, both, near, far, rates, jumps)
    return finish(ends, end, both)[None]


def solution(mesh):
    in_specs = (P("tm", None, "space", None, None), P("space", None, None), P("space", None, None))
    out_specs = P("tm", None, "space", None, None)
    return jax.shard_map(body, mesh=mesh, in_specs=in_specs, out_specs=out_specs, check_vma=False)
```
